256 devices in a mesh: segment: 4 (over z_hi, core), ctx: 16 (over x, z_lo), dp: 4 (over y).
Axes of the slice: x: 4, y: 4, z: 8 (z_hi: 2, z_lo: 4; z = z_hi * 4 + z_lo), core: 2. Of those that a mesh axis runs over, the one named last changes fastest.
Arguments:
- qkv: bfloat16 [4, 4, 2560, 3, 2560], P('segment', 'dp', 'ctx'), may hold values from -24 to 24
- qk_gain: float32 [4, 2, 2560], P('segment'), may hold values from 1.5 to 2.5
- mod_weight: float32 [4, 256, 2560], P('segment'), may hold values from -0.375 to 0.375
- positions: int32 [4, 2560], P('dp', 'ctx'), may hold values from 0 to 75599
- timesteps: int32 [4, 4], P('segment', 'dp'), may hold values from 0 to 999
- cotangent: bfloat16 [4, 4, 2560, 2560], P('segment', 'dp', 'ctx'), may hold values from -6 to 6
Outputs:
- attn_out: bfloat16 [4, 4, 2560, 2560], P('segment', 'dp', 'ctx')
- gate_grad: float32 [4, 256, 2560], P('segment', ('ctx', 'dp'))
The draws below stay inside these ranges and needn't reach their ends.
All inputs are finite; a program needn't handle non-finite values.
Results may differ from the reference program's by a relative error of at most 0.012.
Values may be sent and summed in bfloat16 or wider, within the bound.
No kernel may reach another device: no remote copies, remote signals or barrier semaphores. Data moves between devices by JAX's collectives and lax.ppermute only.
A program may use at most 128 MiB of HBM per device.

```python
import jax
import jax.numpy as jnp
from jax import lax

HEADS = 20
HEAD_DIM = 128
FREQS = 256
GRID_ROWS = 45
GRID_COLS = 80
FRAMES = 21
STEPS = 1000
TOKENS = 2560
HW = 2560
N_SEGMENT = 4
N_DP = 4


def draw_qkv(key, part):
    width = HEADS * HEAD_DIM
    shape = (N_SEGMENT, N_DP, TOKENS, 3, width)
    streams = jax.random.split(jax.random.fold_in(key, 11), 1)
    base = jax.random.normal(streams[0], shape, jnp.float32)
    return jnp.clip(base, -24.0, 24.0).astype(jnp.bfloat16)


def with_ends(values, key, low, largest):
    index_at = [jax.random.randint(jax.random.fold_in(key, axis), (), 0, length) for axis, length in enumerate(values.shape)]
    main_axis = values.shape.index(max(values.shape))
    next_to = index_at[:main_axis] + [(index_at[main_axis] + 1) % values.shape[main_axis]] + index_at[main_axis + 1:]
    return values.at[tuple(index_at)].set(low).at[tuple(next_to)].set(largest)


def shard_levels(stream_key, shape, shards, least, high):
    level, own = 1.0, jax.random.fold_in(stream_key, 6)
    for axis_at, parts in shards:
        heights = jnp.exp(jax.random.uniform(jax.random.fold_in(own, axis_at), (parts,), jnp.float32, least / len(shards), high / len(shards)))
        level = level * jnp.repeat(heights, shape[axis_at] // parts).reshape([-1 if axis == axis_at else 1 for axis in range(len(shape))])
    return level


def bell_draw(key, extent, scale, most, cuts=(), kind=jnp.bfloat16):
    values = jax.random.normal(key, extent, jnp.float32) * scale
    if len(cuts) > 0:
        values = shard_levels(key, extent, cuts, -0.22, 0.18) * values
    return jnp.clip(values, min=-most, max=most).astype(kind)


def setup_inputs(seed: int = 0) -> dict:
    arg_keys = jax.random.split(jax.random.key(seed), 7)
    qkv = draw_qkv(jax.random.fold_in(arg_keys[6], 71), 0)
    qk_gain = jnp.clip(1.5 + 1.0 * jax.random.uniform(arg_keys[1], (N_SEGMENT, 2, HW), jnp.float32) ** shard_levels(arg_keys[1], (N_SEGMENT, 2, HW), ((0, 4),), -0.2, 0.2), 1.5, 2.5)
    mod_weight = bell_draw(arg_keys[2], (N_SEGMENT, FREQS, HW), FREQS ** -0.5, 0.375, ((0, 4),), jnp.float32)
    positions = with_ends(jax.random.randint(arg_keys[3], (N_DP, TOKENS), 0, FRAMES * GRID_ROWS * GRID_COLS), jax.random.fold_in(arg_keys[3], 1), 0, (FRAMES * GRID_ROWS * GRID_COLS) - 1).astype(jnp.int32)
    timesteps = with_ends(jax.random.randint(arg_keys[4], (N_SEGMENT, N_DP), 0, STEPS), jax.random.fold_in(arg_keys[4], 1), 0, STEPS - 1).astype(jnp.int32)
    cotangent = bell_draw(arg_keys[5], (N_SEGMENT, N_DP, TOKENS, HW), 1.0, 6.0, ((0, 4), (1, 4), (2, 16)))
    return {"qkv": qkv, "qk_gain": qk_gain, "mod_weight": mod_weight, "positions": positions, "timesteps": timesteps, "cotangent": cotangent}


def rope_tables(pos):
    half = HEAD_DIM // 2
    side = HEAD_DIM // 6
    first = half - 2 * side
    frame = (pos // (GRID_ROWS * GRID_COLS)).astype(jnp.float32)
    row = (pos // GRID_COLS % GRID_ROWS).astype(jnp.float32)
    col = (pos % GRID_COLS).astype(jnp.float32)
    pair = jnp.arange(half, dtype=jnp.int32)
    group = jnp.where(pair < first, 0, jnp.where(pair < first + side, 1, 2))
    offset = jnp.where(group == 0, 0, jnp.where(group == 1, first, first + side))
    pairs_in = jnp.where(group == 0, first, side).astype(jnp.float32)
    freq = 10000.0 ** (-(pair - offset).astype(jnp.float32) / pairs_in)
    coord = jnp.where(group[None, :] == 0, frame[:, None], jnp.where(group[None, :] == 1, row[:, None], col[:, None]))
    angle = coord * freq[None, :]
    cosine = jnp.tile(jnp.concatenate([jnp.cos(angle), jnp.cos(angle)], axis=1), (1, HEADS))
    sine = jnp.tile(jnp.concatenate([jnp.sin(angle), jnp.sin(angle)], axis=1), (1, HEADS))
    return (cosine, sine)

def rotate(values, cosine, sine):
    count = values.shape[0]
    half = HEAD_DIM // 2
    shaped = values.reshape(count, HEADS, HEAD_DIM)
    turned = jnp.concatenate([-shaped[:, :, half:], shaped[:, :, :half]], axis=2).reshape(count, HEADS * HEAD_DIM)
    return values * cosine + turned * sine

def normalize(values, gain):
    mean_sq = lax.optimization_barrier(jnp.mean(values * values, axis=-1, keepdims=True))
    return values * lax.rsqrt(mean_sq + 1e-06) * gain

def embed(step):
    count = FREQS // 2
    freq = 10000.0 ** (-jnp.arange(count, dtype=jnp.float32) / count)
    angle = step.astype(jnp.float32) * freq
    return jnp.concatenate([jnp.cos(angle), jnp.sin(angle)])

def attention(queries, keys, values):
    count = queries.shape[0]
    qh = queries.astype(jnp.float32).reshape(count, HEADS, HEAD_DIM).transpose(1, 0, 2)
    kh = keys.astype(jnp.float32).reshape(count, HEADS, HEAD_DIM).transpose(1, 0, 2)
    vh = values.astype(jnp.float32).reshape(count, HEADS, HEAD_DIM).transpose(1, 0, 2)
    scale = 1.0 / HEAD_DIM ** 0.5

    def one_head(operands):
        qone, kone, vone = operands
        scores = jnp.dot(qone, kone.T, precision=lax.Precision.HIGHEST) * scale
        peak = lax.optimization_barrier(jnp.max(scores, axis=1, keepdims=True))
        expo = jnp.exp(scores - peak)
        total = lax.optimization_barrier(jnp.sum(expo, axis=1, keepdims=True))
        rounded = expo.astype(jnp.bfloat16).astype(jnp.float32)
        return jnp.dot(rounded, vone, precision=lax.Precision.HIGHEST) / total
    result = lax.map(one_head, (qh, kh, vh))
    return result.transpose(1, 0, 2).reshape(count, HEADS * HEAD_DIM)

def reference(qkv, qk_gain, mod_weight, positions, timesteps, cotangent):
    source = jnp.roll(qkv, 1, axis=0)
    outs = []
    grads = []
    for segment_idx in range(N_SEGMENT):
        segment_outs = []
        grad_sum = jnp.zeros((FREQS, HEADS * HEAD_DIM), jnp.float32)
        for clip_idx in range(N_DP):
            block = source[segment_idx, clip_idx].astype(jnp.float32)
            cosine, sine = rope_tables(positions[clip_idx])
            queries = rotate(normalize(block[:, 0], qk_gain[segment_idx, 0]), cosine, sine).astype(jnp.bfloat16)
            keys = rotate(normalize(block[:, 1], qk_gain[segment_idx, 1]), cosine, sine).astype(jnp.bfloat16)
            values = source[segment_idx, clip_idx, :, 2]
            attn = attention(queries, keys, values)
            emb = embed(timesteps[segment_idx, clip_idx])
            gate = jnp.dot(emb, mod_weight[segment_idx], precision=lax.Precision.HIGHEST)
            segment_outs.append((attn * gate).astype(jnp.bfloat16))
            chan = lax.optimization_barrier(jnp.sum(attn * cotangent[segment_idx, clip_idx].astype(jnp.float32), axis=0))
            grad_sum = grad_sum + emb[:, None] * chan[None, :]
        outs.append(jnp.stack(segment_outs))
        grads.append(grad_sum)
    return (jnp.stack(outs), jnp.stack(grads))
```

```python
import functools

import jax
import jax.numpy as jnp
from jax import lax
from jax.experimental import pallas as pl
from jax.experimental.pallas import tpu as pltpu
from jax.sharding import PartitionSpec as P

HEADS = 20
HEAD_DIM = 128
FREQS = 256
GRID_ROWS = 45
GRID_COLS = 80
SIDE = 4
GROUP = HEADS // SIDE
TOK = 160
ROWS = SIDE * TOK
WIDTH = HEADS * HEAD_DIM
TILE = 320
EXP_SCALE = 1.4426950408889634 / HEAD_DIM**0.5
VMEM = pltpu.CompilerParams(vmem_limit_bytes=56 * 1024 * 1024)
SMEM_SPEC = pl.BlockSpec(memory_space=pltpu.SMEM)
VMEM_SPEC = pl.BlockSpec(memory_space=pltpu.VMEM)


def along_z(value, by):
    pairs = [(i, i // SIDE * SIDE + (i + by) % SIDE) for i in range(SIDE * SIDE)]
    return lax.ppermute(value, "ctx", pairs)


def along_x(value, by):
    pairs = [(i, (i + SIDE * by) % (SIDE * SIDE)) for i in range(SIDE * SIDE)]
    return lax.ppermute(value, "ctx", pairs)


def along_dp(value, by):
    return lax.ppermute(value, "dp", [(i, (i + by) % SIDE) for i in range(SIDE)])


def home(value, by):
    count = SIDE * SIDE
    pairs = []
    for seg in range(SIDE):
        for i in range(count):
            target = (seg + 1) % SIDE * count + i // SIDE * SIDE + (i + by) % SIDE
            pairs.append((seg * count + i, target))
    return lax.ppermute(value, ("segment", "ctx"), pairs)


def rope_tables(pos):
    half = HEAD_DIM // 2
    side = HEAD_DIM // 6
    first = half - 2 * side
    frame = (pos // (GRID_ROWS * GRID_COLS)).astype(jnp.float32)
    row = (pos // GRID_COLS % GRID_ROWS).astype(jnp.float32)
    col = (pos % GRID_COLS).astype(jnp.float32)
    pair = jnp.arange(half, dtype=jnp.int32)
    group = jnp.where(pair < first, 0, jnp.where(pair < first + side, 1, 2))
    offset = jnp.where(group == 0, 0, jnp.where(group == 1, first, first + side))
    pairs_in = jnp.where(group == 0, first, side).astype(jnp.float32)
    freq = 10000.0 ** (-(pair - offset).astype(jnp.float32) / pairs_in)
    coord = jnp.where(
        group[None, :] == 0,
        frame[:, None],
        jnp.where(group[None, :] == 1, row[:, None], col[:, None]),
    )
    angle = coord * freq[None, :]
    cosine = jnp.concatenate([jnp.cos(angle), jnp.cos(angle)], axis=1)
    sine = jnp.concatenate([-jnp.sin(angle), jnp.sin(angle)], axis=1)
    return (cosine, sine)


def call(kernel, out_shape, flops, moved, *operands, smem=1):
    specs = [SMEM_SPEC] * smem + [VMEM_SPEC] * (len(operands) - smem)
    return pl.pallas_call(
        kernel,
        out_shape=out_shape,
        in_specs=specs,
        out_specs=jax.tree.map(lambda _: VMEM_SPEC, out_shape),
        compiler_params=VMEM,
        cost_estimate=pl.CostEstimate(flops=flops, bytes_accessed=moved, transcendentals=0),
    )(*operands)


def column(index):
    return pl.ds(pl.multiple_of(index * HEAD_DIM, HEAD_DIM), HEAD_DIM)


def prep_kernel(z_ref, qkv_ref, gain_ref, cos_ref, sin_ref, *outs):
    z = z_ref[0]
    cosine = cos_ref[...]
    sine = sin_ref[...]
    for part in range(2):
        total = jnp.zeros((TOK, HEAD_DIM), jnp.float32)
        for head in range(HEADS):
            x = qkv_ref[part, :, head * HEAD_DIM : (head + 1) * HEAD_DIM].astype(jnp.float32)
            total = total + x * x
        mean_sq = jnp.sum(total, axis=1, keepdims=True) / WIDTH
        inverse = lax.rsqrt(mean_sq + 1e-06)
        for step in range(SIDE):
            first = lax.rem(z + step, SIDE) * GROUP
            for head in range(GROUP):
                cols = column(first + head)
                x = qkv_ref[part, :, cols].astype(jnp.float32)
                y = x * inverse * gain_ref[part : part + 1, cols]
                turned = pltpu.roll(y, HEAD_DIM // 2, 1)
                y = y * cosine + turned * sine
                outs[step][part * GROUP + head] = y.astype(jnp.bfloat16)
    for step in range(SIDE):
        first = lax.rem(z + step, SIDE) * GROUP
        for head in range(GROUP):
            outs[step][2 * GROUP + head] = qkv_ref[2, :, column(first + head)]


def split_kernel(x_ref, r0, r1, r2, r3, *outs):
    x = x_ref[0]
    last = GROUP - 1
    for j, r in enumerate((r0, r1, r2, r3)):
        rows = pl.ds(j * TOK, TOK)
        for step in range(SIDE):
            head = lax.rem(x + step, SIDE)
            out = outs[step]
            out[0, rows] = r[head]
            out[1, rows] = r[GROUP + head]
            out[2, rows] = r[2 * GROUP + head]
            out[3, rows] = r[GROUP + last]
            out[4, rows] = r[2 * GROUP + last]
        outs[SIDE][rows] = r[last]


def attend(q, blocks, keys_at, values_at):
    nt = (((1,), (1,)), ((), ()))
    scores = [
        lax.dot_general(q, b[keys_at], nt, preferred_element_type=jnp.float32) for b in blocks
    ]
    peak = functools.reduce(jnp.maximum, [jnp.max(s, axis=1, keepdims=True) for s in scores])
    expo = [jnp.exp2((s - peak) * EXP_SCALE) for s in scores]
    total = sum(jnp.sum(e, axis=1, keepdims=True) for e in expo)
    accum = sum(
        jnp.dot(e.astype(jnp.bfloat16), b[values_at], preferred_element_type=jnp.float32)
        for e, b in zip(expo, blocks, strict=True)
    )
    return (accum / total).astype(jnp.bfloat16)


def attention_kernel(t0, t1, t2, t3, shared_ref, *outs):
    blocks = (t0, t1, t2, t3)

    def tile(i, _):
        rows = pl.ds(pl.multiple_of(i * TILE, TILE), TILE)
        for step in range(SIDE):
            outs[step][rows] = attend(blocks[step][0, rows], blocks, 1, 2)
        outs[SIDE][rows] = attend(shared_ref[rows], blocks, 3, 4)
        return 0

    lax.fori_loop(0, ROWS // TILE, tile, 0)


def join_kernel(x_ref, o0, o1, o2, o3, shared_ref, *outs):
    x = x_ref[0]
    for j in range(SIDE):
        rows = pl.ds(j * TOK, TOK)
        for step, o in enumerate((o0, o1, o2, o3)):
            outs[j][:, column(lax.rem(x + step, SIDE))] = o[rows]
        outs[j][:, (GROUP - 1) * HEAD_DIM :] = shared_ref[rows]


def finish_kernel(z_ref, a0, a1, a2, a3, gate_ref, cot_ref, out_ref, chan_ref):
    z = z_ref[0]
    wide = GROUP * HEAD_DIM
    for step, a in enumerate((a0, a1, a2, a3)):
        cols = pl.ds(pl.multiple_of(lax.rem(z + step, SIDE) * wide, HEAD_DIM), wide)
        attn = a[...].astype(jnp.float32)
        out_ref[:, cols] = (attn * gate_ref[:, cols]).astype(jnp.bfloat16)
        chan_ref[:, cols] = jnp.sum(
            attn * cot_ref[:, cols].astype(jnp.float32), axis=0, keepdims=True
        )


def shape(dims, dtype=jnp.bfloat16):
    return jax.ShapeDtypeStruct(dims, dtype)


def frequencies():
    count = FREQS // 2
    return 10000.0 ** (-jnp.arange(count, dtype=jnp.float32) / count)


def embed(step):
    angle = step.astype(jnp.float32) * frequencies()
    return jnp.concatenate([jnp.cos(angle), jnp.sin(angle)])


def local(qkv, qk_gain, mod_weight, positions, timesteps, cotangent):
    ctx = lax.axis_index("ctx").astype(jnp.int32)
    x = (ctx // SIDE)[None]
    z = (ctx % SIDE)[None]
    gains = lax.ppermute(qk_gain[0], "segment", [((i + 1) % SIDE, i) for i in range(SIDE)])
    cosine, sine = rope_tables(positions[0])
    parts = qkv[0, 0].transpose(1, 0, 2)
    sent = call(
        prep_kernel,
        [shape((3 * GROUP, TOK, HEAD_DIM))] * SIDE,
        10_000_000,
        5_000_000,
        z,
        parts,
        gains,
        cosine,
        sine,
    )
    blocks = [sent[0]] + [along_z(sent[k], k) for k in (1, 2, 3)]
    split = call(
        split_kernel,
        [shape((GROUP, ROWS, HEAD_DIM))] * SIDE + [shape((ROWS, HEAD_DIM))],
        0,
        6_000_000,
        x,
        *blocks,
    )
    held = [split[0]] + [along_x(split[m], m) for m in (1, 2, 3)]
    heads = call(
        attention_kernel,
        [shape((ROWS, HEAD_DIM))] * (SIDE + 1),
        4_200_000_000,
        5_000_000,
        *held,
        split[SIDE],
        smem=0,
    )
    back = [heads[0]] + [along_x(heads[m], SIDE - m) for m in (1, 2, 3)]
    joined = call(
        join_kernel,
        [shape((TOK, GROUP * HEAD_DIM))] * SIDE,
        0,
        2_000_000,
        x,
        *back,
        heads[SIDE],
    )
    at_home = [home(joined[k], SIDE - k) for k in range(SIDE)]

    step = timesteps[0, 0]
    emb = embed(step)
    gate = jnp.dot(emb, mod_weight[0], precision=lax.Precision.HIGHEST)
    attn_out, chan = call(
        finish_kernel,
        [shape((TOK, WIDTH)), shape((1, WIDTH), jnp.float32)],
        2_000_000,
        3_000_000,
        z,
        *at_home,
        gate[None],
        cotangent[0, 0],
    )
    chan = chan.reshape(HEADS, HEAD_DIM)
    chan = chan + along_x(chan, 1) + along_x(chan, 2) + along_x(chan, 3)
    chan = chan + along_z(chan, 1) + along_z(chan, 2) + along_z(chan, 3)
    when = jnp.full((1, HEAD_DIM), step.astype(jnp.float32))
    mine = jnp.concatenate([chan, when])
    clips = [mine] + [along_dp(mine, k) for k in (1, 2, 3)]

    rows = FREQS // (SIDE * SIDE * SIDE)
    index = (ctx * SIDE + lax.axis_index("dp").astype(jnp.int32)) * rows
    freq = lax.dynamic_slice_in_dim(jnp.tile(frequencies(), 2), index, rows)
    grad = 0.0
    for clip in clips:
        angle = clip[HEADS, 0] * freq
        part = jnp.where(index < FREQS // 2, jnp.cos(angle), jnp.sin(angle))
        grad = grad + part[:, None] * clip[:HEADS].reshape(1, WIDTH)
    return (attn_out[None, None], grad[None])


def solution(mesh):
    return jax.shard_map(
        local,
        mesh=mesh,
        in_specs=(
            P("segment", "dp", "ctx", None, None),
            P("segment", None, None),
            P("segment", None, None),
            P("dp", "ctx"),
            P("segment", "dp"),
            P("segment", "dp", "ctx", None),
        ),
        out_specs=(P("segment", "dp", "ctx", None), P("segment", ("ctx", "dp"), None)),
        check_vma=False,
    )
```

```python
import functools

import jax
import jax.numpy as jnp
from jax import lax
from jax.experimental import pallas as pl
from jax.experimental.pallas import tpu as pltpu
from jax.sharding import PartitionSpec as P

HEADS = 20
HEAD_DIM = 128
FREQS = 256
GRID_ROWS = 45
GRID_COLS = 80
SIDE = 4
GROUP = HEADS // SIDE
TOK = 160
ROWS = SIDE * TOK
WIDTH = HEADS * HEAD_DIM
TILE = 320
EXP_SCALE = 1.4426950408889634 / HEAD_DIM**0.5
VMEM = pltpu.CompilerParams(vmem_limit_bytes=56 * 1024 * 1024)
SMEM_SPEC = pl.BlockSpec(memory_space=pltpu.SMEM)
VMEM_SPEC = pl.BlockSpec(memory_space=pltpu.VMEM)


def along_z(value, by):
    pairs = [(i, i // SIDE * SIDE + (i + by) % SIDE) for i in range(SIDE * SIDE)]
    return lax.ppermute(value, "ctx", pairs)


def along_x(value, by):
    pairs = [(i, (i + SIDE * by) % (SIDE * SIDE)) for i in range(SIDE * SIDE)]
    return lax.ppermute(value, "ctx", pairs)


def along_dp(value, by):
    return lax.ppermute(value, "dp", [(i, (i + by) % SIDE) for i in range(SIDE)])


def section_pairs(turn, by):
    count = SIDE * SIDE
    pairs = []
    for seg in range(SIDE):
        for i in range(count):
            target = (seg + turn) % SIDE * count + i // SIDE * SIDE + (i + by) % SIDE
            pairs.append((seg * count + i, target))
    return pairs


def home(value, by):
    return lax.ppermute(value, ("segment", "ctx"), section_pairs(1, by))


def away(value, by):
    return lax.ppermute(value, ("segment", "ctx"), section_pairs(SIDE - 1, by))


def rope_tables(pos):
    half = HEAD_DIM // 2
    side = HEAD_DIM // 6
    first = half - 2 * side
    frame = (pos // (GRID_ROWS * GRID_COLS)).astype(jnp.float32)
    row = (pos // GRID_COLS % GRID_ROWS).astype(jnp.float32)
    col = (pos % GRID_COLS).astype(jnp.float32)
    pair = jnp.arange(half, dtype=jnp.int32)
    group = jnp.where(pair < first, 0, jnp.where(pair < first + side, 1, 2))
    offset = jnp.where(group == 0, 0, jnp.where(group == 1, first, first + side))
    pairs_in = jnp.where(group == 0, first, side).astype(jnp.float32)
    freq = 10000.0 ** (-(pair - offset).astype(jnp.float32) / pairs_in)
    coord = jnp.where(
        group[None, :] == 0,
        frame[:, None],
        jnp.where(group[None, :] == 1, row[:, None], col[:, None]),
    )
    angle = coord * freq[None, :]
    cosine = jnp.concatenate([jnp.cos(angle), jnp.cos(angle)], axis=1)
    sine = jnp.concatenate([-jnp.sin(angle), jnp.sin(angle)], axis=1)
    return (cosine, sine)


def call(kernel, out_shape, flops, moved, *operands, smem=1):
    specs = [SMEM_SPEC] * smem + [VMEM_SPEC] * (len(operands) - smem)
    return pl.pallas_call(
        kernel,
        out_shape=out_shape,
        in_specs=specs,
        out_specs=jax.tree.map(lambda _: VMEM_SPEC, out_shape),
        compiler_params=VMEM,
        cost_estimate=pl.CostEstimate(flops=flops, bytes_accessed=moved, transcendentals=0),
    )(*operands)


def group_columns(index):
    wide = GROUP * HEAD_DIM
    return pl.ds(pl.multiple_of(lax.rem(index, SIDE) * wide, HEAD_DIM), wide)


def after(value, first):
    return lax.optimization_barrier((value, first))[0]


def column(index):
    return pl.ds(pl.multiple_of(index * HEAD_DIM, HEAD_DIM), HEAD_DIM)


def prep_kernel(z_ref, qkv_ref, gain_ref, cos_ref, sin_ref, *outs):
    z = z_ref[0]
    cosine = cos_ref[...]
    sine = sin_ref[...]
    for part in (1, 0):
        total = jnp.zeros((TOK, HEAD_DIM), jnp.float32)
        for head in range(HEADS):
            x = qkv_ref[part, :, head * HEAD_DIM : (head + 1) * HEAD_DIM].astype(jnp.float32)
            total = total + x * x
        mean_sq = jnp.sum(total, axis=1, keepdims=True) / WIDTH
        inverse = lax.rsqrt(mean_sq + 1e-06)
        for step in range(SIDE):
            first = lax.rem(z + step, SIDE) * GROUP
            for head in range(GROUP):
                cols = column(first + head)
                x = qkv_ref[part, :, cols].astype(jnp.float32)
                y = x * inverse * gain_ref[part : part + 1, cols]
                turned = pltpu.roll(y, HEAD_DIM // 2, 1)
                y = y * cosine + turned * sine
                outs[(1 - part) * SIDE + step][head] = y.astype(jnp.bfloat16)


def cut_values_kernel(z_ref, v_ref, *outs):
    z = z_ref[0]
    for step in range(SIDE):
        first = lax.rem(z + step, SIDE) * GROUP
        for head in range(GROUP):
            outs[step][head] = v_ref[0, :, column(first + head)]


def cut_cotangent_kernel(z_ref, cot_ref, *outs):
    z = z_ref[0]
    for step in range(SIDE):
        outs[step][...] = cot_ref[:, group_columns(z + step)]


def split_pairs_kernel(x_ref, r0, r1, r2, r3, *outs):
    x = x_ref[0]
    for j, r in enumerate((r0, r1, r2, r3)):
        rows = pl.ds(j * TOK, TOK)
        for step in range(SIDE):
            outs[step][0, rows] = r[lax.rem(x + step, SIDE)]
            outs[step][1, rows] = r[GROUP - 1]


def split_queries_kernel(x_ref, r0, r1, r2, r3, *outs):
    x = x_ref[0]
    for j, r in enumerate((r0, r1, r2, r3)):
        rows = pl.ds(j * TOK, TOK)
        for step in range(SIDE):
            outs[step][rows] = r[lax.rem(x + step, SIDE)]
        outs[SIDE][rows] = r[GROUP - 1]


def attention_kernel(which, q_ref, k0, k1, k2, k3, v0, v1, v2, v3, out_ref):
    keys = (k0, k1, k2, k3)
    values = (v0, v1, v2, v3)
    nt = (((1,), (1,)), ((), ()))
    for i in range(ROWS // TILE):
        rows = pl.ds(i * TILE, TILE)
        q = q_ref[rows]
        scores = [
            lax.dot_general(q, k[which], nt, preferred_element_type=jnp.float32) for k in keys
        ]
        peak = functools.reduce(jnp.maximum, [jnp.max(s, axis=1, keepdims=True) for s in scores])
        expo = [jnp.exp2((s - peak) * EXP_SCALE) for s in scores]
        total = sum(jnp.sum(e, axis=1, keepdims=True) for e in expo)
        accum = sum(
            jnp.dot(e.astype(jnp.bfloat16), v[which], preferred_element_type=jnp.float32)
            for e, v in zip(expo, values, strict=True)
        )
        out_ref[rows] = (accum / total).astype(jnp.bfloat16)


def join_kernel(x_ref, *refs):
    x = x_ref[0]
    heads = refs[:SIDE]
    shared_ref = refs[SIDE]
    cots = refs[SIDE + 1 : 2 * SIDE + 1]
    outs = refs[2 * SIDE + 1 : 3 * SIDE + 1]
    chan_ref = refs[3 * SIDE + 1]
    chan_ref[...] = jnp.zeros_like(chan_ref)
    for step in range(GROUP):
        source = heads[step] if step < SIDE else shared_ref
        place = lax.rem(x + step, SIDE) if step < SIDE else SIDE
        cols = column(place)
        total = jnp.zeros((TOK, HEAD_DIM), jnp.float32)
        for j in range(SIDE):
            o = source[j * TOK : (j + 1) * TOK]
            outs[j][:, cols] = o
            total = total + o.astype(jnp.float32) * cots[j][:, cols].astype(jnp.float32)
        chan_ref[pl.ds(place, 1)] = jnp.sum(total, axis=0, keepdims=True)


def finish_kernel(z_ref, a0, a1, a2, a3, gate_ref, out_ref):
    z = z_ref[0]
    for step, a in enumerate((a0, a1, a2, a3)):
        cols = group_columns(z + step)
        out_ref[:, cols] = (a[...].astype(jnp.float32) * gate_ref[:, cols]).astype(jnp.bfloat16)


def grad_kernel(z_ref, part_ref, c0, c1, c2, c3, out_ref):
    z = z_ref[0]
    for step in range(SIDE):
        first = lax.rem(z + step, SIDE) * GROUP
        for head in range(GROUP):
            total = 0.0
            for d, c in enumerate((c0, c1, c2, c3)):
                total = total + part_ref[d] * c[step, head : head + 1]
            out_ref[:, column(first + head)] = total


def shape(dims, dtype=jnp.bfloat16):
    return jax.ShapeDtypeStruct(dims, dtype)


def frequencies():
    count = FREQS // 2
    return 10000.0 ** (-jnp.arange(count, dtype=jnp.float32) / count)


def embed(step):
    angle = step.astype(jnp.float32) * frequencies()
    return jnp.concatenate([jnp.cos(angle), jnp.sin(angle)])


def attention(which, q, keys, values):
    return call(
        functools.partial(attention_kernel, which),
        shape((ROWS, HEAD_DIM)),
        840_000_000,
        1_600_000,
        q,
        *keys,
        *values,
        smem=0,
    )


def local(qkv, qk_gain, mod_weight, positions, timesteps, cotangent):
    ctx = lax.axis_index("ctx").astype(jnp.int32)
    x = (ctx // SIDE)[None]
    z = (ctx % SIDE)[None]
    steps = (1, 2, 3)
    block = shape((GROUP, TOK, HEAD_DIM))
    pair = shape((2, ROWS, HEAD_DIM))
    single = shape((ROWS, HEAD_DIM))
    flat = shape((TOK, GROUP * HEAD_DIM))

    gains = lax.ppermute(qk_gain[0], "segment", [((i + 1) % SIDE, i) for i in range(SIDE)])
    parts = qkv[0, 0].transpose(1, 0, 2)
    values = call(cut_values_kernel, [block] * SIDE, 0, 1_600_000, z, parts[2:])
    values_z = [values[0]] + [along_z(values[k], k) for k in steps]
    cosine, sine = rope_tables(positions[0])
    turned = call(
        prep_kernel, [block] * (2 * SIDE), 10_000_000, 3_500_000, z, parts, gains, cosine, sine
    )
    keys, queries = turned[:SIDE], turned[SIDE:]
    keys_z = [keys[0]] + [along_z(after(keys[k], values_z[k]), k) for k in steps]
    values_s = call(split_pairs_kernel, [pair] * SIDE, 0, 2_500_000, x, *values_z)
    values_x = [values_s[0]] + [along_x(values_s[m], m) for m in steps]
    queries_z = [queries[0]] + [along_z(after(queries[k], keys_z[k]), k) for k in steps]
    keys_s = call(split_pairs_kernel, [pair] * SIDE, 0, 2_500_000, x, *keys_z)
    keys_x = [keys_s[0]] + [along_x(after(keys_s[m], values_x[m]), m) for m in steps]
    queries_s = call(split_queries_kernel, [single] * GROUP, 0, 1_600_000, x, *queries_z)
    queries_x = [queries_s[0]] + [along_x(after(queries_s[m], keys_x[m]), m) for m in steps]

    cots = call(cut_cotangent_kernel, [flat] * SIDE, 0, 1_600_000, z, cotangent[0, 0])
    cots_z = [away(after(cots[k], queries_z[max(k, 1)]), k) for k in range(SIDE)]

    shared = attention(1, queries_s[SIDE], keys_x, values_x)
    heads = [attention(0, queries_x[m], keys_x, values_x) for m in range(SIDE)]
    back = [heads[0]] + [along_x(heads[m], SIDE - m) for m in steps]
    *joined, chan = call(
        join_kernel,
        [flat] * SIDE + [shape((8, HEAD_DIM), jnp.float32)],
        2_000_000,
        2_500_000,
        x,
        *back,
        shared,
        *cots_z,
    )
    at_home = [home(joined[k], (SIDE - k) % SIDE) for k in range(SIDE)]

    chan = chan + along_x(chan, 1) + along_x(chan, 2) + along_x(chan, 3)
    mine = jnp.stack([home(chan, (SIDE - k) % SIDE) for k in range(SIDE)])
    step = timesteps[0, 0]
    mine = mine.at[:, GROUP].set(step.astype(jnp.float32))
    clips = [mine] + [along_dp(mine, k) for k in steps]
    rows = FREQS // (SIDE * SIDE * SIDE)
    index = (ctx * SIDE + lax.axis_index("dp").astype(jnp.int32)) * rows
    freq = lax.dynamic_slice_in_dim(jnp.tile(frequencies(), 2), index, rows)
    angle = jnp.stack([clip[0, GROUP, 0] for clip in clips])[:, None] * freq
    factors = jnp.where(index < FREQS // 2, jnp.cos(angle), jnp.sin(angle))
    grad = call(
        grad_kernel,
        shape((rows, WIDTH), jnp.float32),
        0,
        200_000,
        z,
        jnp.broadcast_to(factors[:, :, None], (SIDE, rows, HEAD_DIM)),
        *clips,
    )

    gate = jnp.dot(embed(step), mod_weight[0], precision=lax.Precision.HIGHEST)
    attn_out = call(
        finish_kernel, shape((TOK, WIDTH)), 500_000, 1_700_000, z, *at_home, gate[None]
    )
    return (attn_out[None, None], grad[None])


def solution(mesh):
    return jax.shard_map(
        local,
        mesh=mesh,
        in_specs=(
            P("segment", "dp", "ctx", None, None),
            P("segment", None, None),
            P("segment", None, None),
            P("dp", "ctx"),
            P("segment", "dp"),
            P("segment", "dp", "ctx", None),
        ),
        out_specs=(P("segment", "dp", "ctx", None), P("segment", ("ctx", "dp"), None)),
        check_vma=False,
    )
```

```python
import functools

import jax
import jax.numpy as jnp
import numpy as np
from jax import lax
from jax.experimental import pallas as pl
from jax.experimental.pallas import tpu as pltpu
from jax.sharding import PartitionSpec as P

HEADS = 20
HEAD_DIM = 128
FREQS = 256
GRID_ROWS = 45
GRID_COLS = 80
SIDE = 4
GROUP = HEADS // SIDE
TOK = 160
ROWS = SIDE * TOK
WIDTH = HEADS * HEAD_DIM
TILE = 320
EXP_SCALE = 1.4426950408889634 / HEAD_DIM**0.5
VMEM = pltpu.CompilerParams(vmem_limit_bytes=56 * 1024 * 1024)
SMEM_SPEC = pl.BlockSpec(memory_space=pltpu.SMEM)
VMEM_SPEC = pl.BlockSpec(memory_space=pltpu.VMEM)


def along_z(value, by):
    pairs = [(i, i // SIDE * SIDE + (i + by) % SIDE) for i in range(SIDE * SIDE)]
    return lax.ppermute(value, "ctx", pairs)


def along_x(value, by):
    pairs = [(i, (i + SIDE * by) % (SIDE * SIDE)) for i in range(SIDE * SIDE)]
    return lax.ppermute(value, "ctx", pairs)


def along_dp(value, by):
    return lax.ppermute(value, "dp", [(i, (i + by) % SIDE) for i in range(SIDE)])


def exchanged(along, blocks):
    got = list(blocks)
    for k in (2, 1, 3):
        got[k] = along(blocks[k], k)
    return got


def section_pairs(turn, by):
    count = SIDE * SIDE
    pairs = []
    for seg in range(SIDE):
        for i in range(count):
            target = (seg + turn) % SIDE * count + i // SIDE * SIDE + (i + by) % SIDE
            pairs.append((seg * count + i, target))
    return pairs


def home(value, by):
    return lax.ppermute(value, ("segment", "ctx"), section_pairs(1, by))


def away(value, by):
    return lax.ppermute(value, ("segment", "ctx"), section_pairs(SIDE - 1, by))


def rope_tables(pos):
    half = HEAD_DIM // 2
    side = HEAD_DIM // 6
    first = half - 2 * side
    frame = (pos // (GRID_ROWS * GRID_COLS)).astype(jnp.float32)
    row = (pos // GRID_COLS % GRID_ROWS).astype(jnp.float32)
    col = (pos % GRID_COLS).astype(jnp.float32)
    pair = np.arange(half)
    group = np.where(pair < first, 0, np.where(pair < first + side, 1, 2))
    offset = np.where(group == 0, 0, np.where(group == 1, first, first + side))
    pairs_in = np.where(group == 0, first, side)
    freq = (10000.0 ** (-(pair - offset) / pairs_in)).astype(np.float32)
    coord = jnp.where(
        group[None, :] == 0,
        frame[:, None],
        jnp.where(group[None, :] == 1, row[:, None], col[:, None]),
    )
    angle = coord * freq[None, :]
    cosine = jnp.concatenate([jnp.cos(angle), jnp.cos(angle)], axis=1)
    sine = jnp.concatenate([-jnp.sin(angle), jnp.sin(angle)], axis=1)
    return (cosine, sine)


def one_of(which, dims):
    return pl.BlockSpec((1, *dims), lambda i: (which, 0, 0))


def call(kernel, out_shape, flops, moved, *operands, smem=1, specs=None):
    grid = () if specs is None else (1,)
    specs = specs or [SMEM_SPEC] * smem + [VMEM_SPEC] * (len(operands) - smem)
    return pl.pallas_call(
        kernel,
        grid=grid,
        out_shape=out_shape,
        in_specs=specs,
        out_specs=jax.tree.map(lambda _: VMEM_SPEC, out_shape),
        compiler_params=VMEM,
        cost_estimate=pl.CostEstimate(flops=0, bytes_accessed=0, transcendentals=0),
    )(*operands)


def group_columns(index):
    wide = GROUP * HEAD_DIM
    return pl.ds(pl.multiple_of(lax.rem(index, SIDE) * wide, HEAD_DIM), wide)


def after(value, first):
    return lax.optimization_barrier((value, first))[0]


def column(index):
    return pl.ds(pl.multiple_of(index * HEAD_DIM, HEAD_DIM), HEAD_DIM)


def prep_kernel(z_ref, qkv_ref, gain_ref, cos_ref, sin_ref, *outs):
    z = z_ref[0]
    cosine = cos_ref[...]
    sine = sin_ref[...]
    for part in (1, 0):
        total = jnp.zeros((TOK, HEAD_DIM), jnp.float32)
        for head in range(HEADS):
            x = qkv_ref[part, :, head * HEAD_DIM : (head + 1) * HEAD_DIM].astype(jnp.float32)
            total = total + x * x
        mean_sq = jnp.sum(total, axis=1, keepdims=True) / WIDTH
        inverse = lax.rsqrt(mean_sq + 1e-06)
        for step in range(SIDE):
            first = lax.rem(z + step, SIDE) * GROUP
            for head in range(GROUP):
                cols = column(first + head)
                x = qkv_ref[part, :, cols].astype(jnp.float32)
                y = x * inverse * gain_ref[part : part + 1, cols]
                turned = pltpu.roll(y, HEAD_DIM // 2, 1)
                y = y * cosine + turned * sine
                outs[(1 - part) * SIDE + step][head] = y.astype(jnp.bfloat16)


def cut_values_kernel(z_ref, v_ref, *outs):
    z = z_ref[0]
    for step in range(SIDE):
        first = lax.rem(z + step, SIDE) * GROUP
        for head in range(GROUP):
            outs[step][head] = v_ref[0, :, column(first + head)]


def cut_cotangent_kernel(z_ref, cot_ref, *outs):
    z = z_ref[0]
    for step in range(SIDE):
        outs[step][...] = cot_ref[:, group_columns(z + step)]


def split_pairs_kernel(x_ref, r0, r1, r2, r3, *outs):
    x = x_ref[0]
    for j, r in enumerate((r0, r1, r2, r3)):
        rows = pl.ds(j * TOK, TOK)
        for step in range(SIDE):
            outs[step][0, rows] = r[lax.rem(x + step, SIDE)]
            outs[step][1, rows] = r[GROUP - 1]


def split_queries_kernel(x_ref, r0, r1, r2, r3, *outs):
    x = x_ref[0]
    for j, r in enumerate((r0, r1, r2, r3)):
        rows = pl.ds(j * TOK, TOK)
        for step in range(SIDE):
            outs[step][rows] = r[lax.rem(x + step, SIDE)]
        outs[SIDE][rows] = r[GROUP - 1]


def attention_kernel(count, *refs):
    queries = refs[:count]
    keys = refs[count : count + SIDE]
    values = refs[count + SIDE : count + 2 * SIDE]
    outs = refs[count + 2 * SIDE :]
    nt = (((1,), (1,)), ((), ()))
    for q_ref, out_ref in zip(queries, outs, strict=True):
        for i in range(ROWS // TILE):
            rows = pl.ds(i * TILE, TILE)
            q = q_ref[rows]
            scores = [
                lax.dot_general(q, k[0], nt, preferred_element_type=jnp.float32) for k in keys
            ]
            peak = functools.reduce(
                jnp.maximum, [jnp.max(s, axis=1, keepdims=True) for s in scores]
            )
            expo = [jnp.exp2((s - peak) * EXP_SCALE) for s in scores]
            total = sum(jnp.sum(e, axis=1, keepdims=True) for e in expo)
            accum = sum(
                jnp.dot(e.astype(jnp.bfloat16), v[0], preferred_element_type=jnp.float32)
                for e, v in zip(expo, values, strict=True)
            )
            out_ref[rows] = (accum / total).astype(jnp.bfloat16)


def join_kernel(x_ref, *refs):
    x = x_ref[0]
    outs = refs[GROUP:]
    for step in range(GROUP):
        place = lax.rem(x + step, SIDE) if step < SIDE else SIDE
        for j in range(SIDE):
            outs[j][:, column(place)] = refs[step][j * TOK : (j + 1) * TOK]


def channels_kernel(x_ref, time_ref, *refs):
    x = x_ref[0]
    cots = refs[GROUP : GROUP + SIDE]
    chan_ref = refs[GROUP + SIDE]
    chan_ref[...] = jnp.zeros_like(chan_ref)
    for step in range(GROUP):
        place = lax.rem(x + step, SIDE) if step < SIDE else SIDE
        total = jnp.zeros((TOK, HEAD_DIM), jnp.float32)
        for j in range(SIDE):
            attn = refs[step][j * TOK : (j + 1) * TOK].astype(jnp.float32)
            total = total + attn * cots[j][:, column(place)].astype(jnp.float32)
        chan_ref[pl.ds(place, 1)] = jnp.sum(total, axis=0, keepdims=True)
    chan_ref[GROUP : GROUP + 1] = time_ref[2:3, :HEAD_DIM]


def finish_kernel(z_ref, a0, a1, a2, a3, gate_ref, out_ref):
    z = z_ref[0]
    for step, a in enumerate((a0, a1, a2, a3)):
        cols = group_columns(z + step)
        out_ref[:, cols] = (a[...].astype(jnp.float32) * gate_ref[:, cols]).astype(jnp.bfloat16)


def grad_kernel(index_ref, freq_ref, chan_ref, out_ref):
    is_cosine = index_ref[0] < FREQS // 2
    factors = []
    for d in range(SIDE):
        angle = chan_ref[d, GROUP : GROUP + 1] * freq_ref[...]
        factors.append(jnp.where(is_cosine, jnp.cos(angle), jnp.sin(angle)))
    for z in range(SIDE):
        chans = [sum(chan_ref[(x * SIDE + z) * SIDE + d] for x in range(SIDE)) for d in range(SIDE)]
        for head in range(GROUP):
            total = sum(f * c[head : head + 1] for f, c in zip(factors, chans, strict=True))
            at = (z * GROUP + head) * HEAD_DIM
            out_ref[:, at : at + HEAD_DIM] = total


def shape(dims, dtype=jnp.bfloat16):
    return jax.ShapeDtypeStruct(dims, dtype)


def frequencies():
    count = FREQS // 2
    return (10000.0 ** (-np.arange(count) / count)).astype(np.float32)


def embed(step):
    angle = step.astype(jnp.float32) * frequencies()
    return jnp.concatenate([jnp.cos(angle), jnp.sin(angle)])


def attention(which, queries, keys, values):
    count = len(queries)
    part = one_of(which, (ROWS, HEAD_DIM))
    return call(
        functools.partial(attention_kernel, count),
        [shape((ROWS, HEAD_DIM))] * count,
        840_000_000 * count,
        1_600_000,
        *queries,
        *keys,
        *values,
        specs=[VMEM_SPEC] * count + [part] * (2 * SIDE),
    )


def local(qkv, qk_gain, mod_weight, positions, timesteps, cotangent):
    ctx = lax.axis_index("ctx").astype(jnp.int32)
    x = (ctx // SIDE)[None]
    z = (ctx % SIDE)[None]
    steps = (1, 2, 3)
    block = shape((GROUP, TOK, HEAD_DIM))
    pair = shape((2, ROWS, HEAD_DIM))
    single = shape((ROWS, HEAD_DIM))
    flat = shape((TOK, GROUP * HEAD_DIM))

    step = timesteps[0, 0]
    when = jnp.full((1, WIDTH), step.astype(jnp.float32))
    gains = jnp.concatenate([qk_gain[0], when])
    gains = lax.ppermute(gains, "segment", [((i + 1) % SIDE, i) for i in range(SIDE)])
    parts = qkv[0, 0].transpose(1, 0, 2)
    values = call(
        cut_values_kernel,
        [block] * SIDE,
        0,
        1_600_000,
        z,
        parts,
        specs=[SMEM_SPEC, one_of(2, (TOK, WIDTH))],
    )
    values_z = exchanged(along_z, values)
    cosine, sine = rope_tables(after(positions[0], values))
    turned = call(
        prep_kernel, [block] * (2 * SIDE), 10_000_000, 3_500_000, z, parts, after(gains, values_z[1]), cosine, sine
    )
    keys, queries = turned[:SIDE], turned[SIDE:]
    keys_z = exchanged(along_z, keys)
    values_s = call(split_pairs_kernel, [pair] * SIDE, 0, 2_500_000, x, *values_z)
    values_x = exchanged(along_x, values_s)
    queries_z = exchanged(along_z, [after(q, keys_z[max(k, 1)]) for k, q in enumerate(queries)])
    keys_s = call(split_pairs_kernel, [pair] * SIDE, 0, 2_500_000, x, *keys_z)
    keys_x = exchanged(along_x, keys_s)
    queries_s = call(
        split_queries_kernel, [single] * GROUP, 0, 1_600_000, x, *after(queries_z, values_x)
    )
    queries_x = exchanged(along_x, queries_s[:SIDE])

    cots = call(cut_cotangent_kernel, [flat] * SIDE, 0, 1_600_000, z, cotangent[0, 0])
    cots_z = [None] * SIDE
    for k in (2, 1, 3, 0):
        cots_z[k] = away(after(cots[k], queries_z[2]), k)

    gate = jnp.dot(embed(step), mod_weight[0], precision=lax.Precision.HIGHEST)[None]
    rows = FREQS // (SIDE * SIDE * SIDE)
    index = (ctx * SIDE + lax.axis_index("dp").astype(jnp.int32)) * rows
    freq = lax.dynamic_slice_in_dim(np.tile(frequencies(), 2), index, rows)
    freq = jnp.broadcast_to(freq[:, None], (rows, HEAD_DIM))
    (shared,) = attention(1, [queries_s[SIDE]], keys_x, values_x)
    queries_x, gate = lax.optimization_barrier((queries_x, gate, shared))[:2]
    (heads2,) = attention(0, [queries_x[2]], keys_x, values_x)
    heads1, heads3 = attention(0, [queries_x[1], queries_x[3]], keys_x, values_x)
    (heads0,) = attention(0, [after(queries_x[0], cots_z)], keys_x, values_x)
    back = [heads0, along_x(heads1, 3), along_x(heads2, 2), along_x(heads3, 1)]
    joined = call(join_kernel, [flat] * SIDE, 0, 1_600_000, x, *back, shared)
    at_home = [None] * SIDE
    for k in (2, 1, 3, 0):
        at_home[k] = home(joined[k], (SIDE - k) % SIDE)
    chan = call(
        channels_kernel,
        shape((8, HEAD_DIM), jnp.float32),
        1_000_000,
        1_600_000,
        x,
        gains,
        *back,
        shared,
        *cots_z,
    )
    count = SIDE * SIDE * SIDE
    chans = jnp.broadcast_to(chan[None], (count, 8, HEAD_DIM))
    chans = lax.all_to_all(chans, ("ctx", "dp"), 0, 0)
    grad = call(
        grad_kernel, shape((rows, WIDTH), jnp.float32), 0, 200_000, index[None], freq, chans
    )
    grad = lax.ppermute(grad, "segment", [(i, (i + 1) % SIDE) for i in range(SIDE)])

    attn_out = call(
        finish_kernel, shape((TOK, WIDTH)), 500_000, 1_700_000, z, *at_home, gate
    )
    return (attn_out[None, None], grad[None])


def solution(mesh):
    return jax.shard_map(
        local,
        mesh=mesh,
        in_specs=(
            P("segment", "dp", "ctx", None, None),
            P("segment", None, None),
            P("segment", None, None),
            P("dp", "ctx"),
            P("segment", "dp"),
            P("segment", "dp", "ctx", None),
        ),
        out_specs=(P("segment", "dp", "ctx", None), P("segment", ("ctx", "dp"), None)),
        check_vma=False,
    )
```

```python
import functools

import jax
import jax.numpy as jnp
import numpy as np
from jax import lax
from jax.experimental import pallas as pl
from jax.experimental.pallas import tpu as pltpu
from jax.sharding import PartitionSpec as P

HEADS = 20
HEAD_DIM = 128
FREQS = 256
GRID_ROWS = 45
GRID_COLS = 80
SIDE = 4
GROUP = HEADS // SIDE
TOK = 160
ROWS = SIDE * TOK
WIDTH = HEADS * HEAD_DIM
TILE = 320
EXP_SCALE = 1.4426950408889634 / HEAD_DIM**0.5
VMEM = pltpu.CompilerParams(vmem_limit_bytes=56 * 1024 * 1024)
SMEM_SPEC = pl.BlockSpec(memory_space=pltpu.SMEM)
VMEM_SPEC = pl.BlockSpec(memory_space=pltpu.VMEM)


def along_z(value, by):
    pairs = [(i, i // SIDE * SIDE + (i + by) % SIDE) for i in range(SIDE * SIDE)]
    return lax.ppermute(value, "ctx", pairs)


def along_x(value, by):
    pairs = [(i, (i + SIDE * by) % (SIDE * SIDE)) for i in range(SIDE * SIDE)]
    return lax.ppermute(value, "ctx", pairs)


def along_dp(value, by):
    return lax.ppermute(value, "dp", [(i, (i + by) % SIDE) for i in range(SIDE)])


def exchanged(along, blocks):
    got = list(blocks)
    for k in (2, 1, 3):
        got[k] = along(blocks[k], k)
    return got


def section_pairs(turn, by):
    count = SIDE * SIDE
    pairs = []
    for seg in range(SIDE):
        for i in range(count):
            target = (seg + turn) % SIDE * count + i // SIDE * SIDE + (i + by) % SIDE
            pairs.append((seg * count + i, target))
    return pairs


def home(value, by):
    return lax.ppermute(value, ("segment", "ctx"), section_pairs(1, by))


def away(value, by):
    return lax.ppermute(value, ("segment", "ctx"), section_pairs(SIDE - 1, by))


def rope_tables(pos):
    half = HEAD_DIM // 2
    side = HEAD_DIM // 6
    first = half - 2 * side
    frame = (pos // (GRID_ROWS * GRID_COLS)).astype(jnp.float32)
    row = (pos // GRID_COLS % GRID_ROWS).astype(jnp.float32)
    col = (pos % GRID_COLS).astype(jnp.float32)
    pair = np.arange(half)
    group = np.where(pair < first, 0, np.where(pair < first + side, 1, 2))
    offset = np.where(group == 0, 0, np.where(group == 1, first, first + side))
    pairs_in = np.where(group == 0, first, side)
    freq = (10000.0 ** (-(pair - offset) / pairs_in)).astype(np.float32)
    coord = jnp.where(
        group[None, :] == 0,
        frame[:, None],
        jnp.where(group[None, :] == 1, row[:, None], col[:, None]),
    )
    angle = coord * freq[None, :]
    cosine = jnp.concatenate([jnp.cos(angle), jnp.cos(angle)], axis=1)
    sine = jnp.concatenate([-jnp.sin(angle), jnp.sin(angle)], axis=1)
    return (cosine, sine)


def one_of(which, dims):
    return pl.BlockSpec((1, *dims), lambda i: (which, 0, 0))


def call(kernel, out_shape, flops, moved, *operands, smem=1, specs=None):
    grid = () if specs is None else (1,)
    specs = specs or [SMEM_SPEC] * smem + [VMEM_SPEC] * (len(operands) - smem)
    return pl.pallas_call(
        kernel,
        grid=grid,
        out_shape=out_shape,
        in_specs=specs,
        out_specs=jax.tree.map(lambda _: VMEM_SPEC, out_shape),
        compiler_params=VMEM,
        cost_estimate=pl.CostEstimate(flops=0, bytes_accessed=0, transcendentals=0),
    )(*operands)


def group_columns(index):
    wide = GROUP * HEAD_DIM
    return pl.ds(pl.multiple_of(lax.rem(index, SIDE) * wide, HEAD_DIM), wide)


def after(value, first):
    return lax.optimization_barrier((value, first))[0]


def column(index):
    return pl.ds(pl.multiple_of(index * HEAD_DIM, HEAD_DIM), HEAD_DIM)


def prep_kernel(z_ref, qkv_ref, gain_ref, cos_ref, sin_ref, main_ref, *shared):
    z = z_ref[0]
    cosine = cos_ref[...]
    sine = sin_ref[...]
    for part in range(3):
        if part < 2:
            total = jnp.zeros((TOK, HEAD_DIM), jnp.float32)
            for head in range(HEADS):
                x = qkv_ref[part, :, head * HEAD_DIM : (head + 1) * HEAD_DIM].astype(jnp.float32)
                total = total + x * x
            mean_sq = jnp.sum(total, axis=1, keepdims=True) / WIDTH
            inverse = lax.rsqrt(mean_sq + 1e-06)

        def head_of(cols):
            x = qkv_ref[part, :, cols]
            if part == 2:
                return x
            y = x.astype(jnp.float32) * inverse * gain_ref[part : part + 1, cols]
            turned = pltpu.roll(y, HEAD_DIM // 2, 1)
            return (y * cosine + turned * sine).astype(jnp.bfloat16)

        for step in range(SIDE):
            shared[step][part] = head_of(column(lax.rem(z + step, SIDE) * GROUP + GROUP - 1))
        for to_x in range(SIDE):
            for to_z in range(SIDE):
                at = (to_z * GROUP + to_x) * HEAD_DIM
                main_ref[to_x * SIDE + to_z, part] = head_of(slice(at, at + HEAD_DIM))


def cut_cotangent_kernel(z_ref, cot_ref, *outs):
    z = z_ref[0]
    for step in range(SIDE):
        outs[step][...] = cot_ref[:, group_columns(z + step)]


def attend(q, keys, values):
    nt = (((1,), (1,)), ((), ()))
    scores = [lax.dot_general(q, k, nt, preferred_element_type=jnp.float32) for k in keys]
    peak = functools.reduce(jnp.maximum, [jnp.max(s, axis=1, keepdims=True) for s in scores])
    expo = [jnp.exp2((s - peak) * EXP_SCALE) for s in scores]
    total = sum(jnp.sum(e, axis=1, keepdims=True) for e in expo)
    accum = sum(
        jnp.dot(e.astype(jnp.bfloat16), v, preferred_element_type=jnp.float32)
        for e, v in zip(expo, values, strict=True)
    )
    return (accum / total).astype(jnp.bfloat16)


def shared_kernel(q0, q1, q2, q3, s0, s1, s2, s3, out_ref):
    blocks = (s0, s1, s2, s3)
    for pair in ((q0, q1), (q2, q3)):
        at = 0 if pair[0] is q0 else TILE
        q = jnp.concatenate([p[0] for p in pair])
        out_ref[at : at + TILE] = attend(q, [b[0] for b in blocks], [b[1] for b in blocks])


def main_kernel(back, x_ref, r_ref, *outs):
    x = x_ref[0]

    def four(part, first):
        return r_ref[pl.ds(first * SIDE, SIDE), part].reshape(ROWS, HEAD_DIM)

    keys = [four(1, m) for m in range(SIDE)]
    values = [four(2, m) for m in range(SIDE)]
    for step, out_ref in zip(back, outs, strict=True):
        first = lax.rem(x + SIDE - step, SIDE) * SIDE
        for i in range(ROWS // TILE):
            half = SIDE // 2
            q = r_ref[pl.ds(first + i * half, half), 0].reshape(TILE, HEAD_DIM)
            out_ref[i * TILE : (i + 1) * TILE] = attend(q, keys, values)


def rows_of(z, source, step):
    first = lax.rem(z + SIDE - step, SIDE) if source < SIDE else step
    return pl.ds(pl.multiple_of(first * TOK, 32), TOK)


def join_kernel(place_ref, *refs):
    x, z = place_ref[0], place_ref[1]
    outs = refs[GROUP:]
    for source in range(GROUP):
        place = lax.rem(x + source, SIDE) if source < SIDE else SIDE
        for step in range(SIDE):
            outs[step][:, column(place)] = refs[source][rows_of(z, source, step)]


def channels_kernel(place_ref, time_ref, *refs):
    x, z = place_ref[0], place_ref[1]
    cots = refs[GROUP : GROUP + SIDE]
    out_ref, chan_ref = refs[GROUP + SIDE :]
    chan_ref[...] = jnp.zeros_like(chan_ref)
    for source in range(GROUP):
        place = lax.rem(x + source, SIDE) if source < SIDE else SIDE
        total = jnp.zeros((TOK, HEAD_DIM), jnp.float32)
        for step in range(SIDE):
            attn = refs[source][rows_of(z, source, step)].astype(jnp.float32)
            total = total + attn * cots[step][:, column(place)].astype(jnp.float32)
        chan_ref[pl.ds(place, 1)] = jnp.sum(total, axis=0, keepdims=True)
    chan_ref[GROUP : GROUP + 1] = time_ref[2:3, :HEAD_DIM]
    for i in range(out_ref.shape[0]):
        out_ref[i] = chan_ref[...]


def finish_kernel(z_ref, a0, a1, a2, a3, gate_ref, out_ref):
    z = z_ref[0]
    for step, a in enumerate((a0, a1, a2, a3)):
        cols = group_columns(z + step)
        out_ref[:, cols] = (a[...].astype(jnp.float32) * gate_ref[:, cols]).astype(jnp.bfloat16)


def grad_kernel(index_ref, freq_ref, before_ref, chan_ref, out_ref):
    is_cosine = index_ref[0] < FREQS // 2
    factors = []
    for d in range(SIDE):
        angle = chan_ref[d, GROUP : GROUP + 1] * freq_ref[...]
        factors.append(jnp.where(is_cosine, jnp.cos(angle), jnp.sin(angle)))
    for z in range(SIDE):
        chans = [sum(chan_ref[(x * SIDE + z) * SIDE + d] for x in range(SIDE)) for d in range(SIDE)]
        for head in range(GROUP):
            total = sum(f * c[head : head + 1] for f, c in zip(factors, chans, strict=True))
            at = (z * GROUP + head) * HEAD_DIM
            cols = slice(at, at + HEAD_DIM)
            out_ref[:, cols] = before_ref[:, cols] + total


def shape(dims, dtype=jnp.bfloat16):
    return jax.ShapeDtypeStruct(dims, dtype)


def frequencies():
    count = FREQS // 2
    return (10000.0 ** (-np.arange(count) / count)).astype(np.float32)


def embed(step):
    angle = step.astype(jnp.float32) * frequencies()
    return jnp.concatenate([jnp.cos(angle), jnp.sin(angle)])


def local(qkv, qk_gain, mod_weight, positions, timesteps, cotangent):
    ctx = lax.axis_index("ctx").astype(jnp.int32)
    x = (ctx // SIDE)[None]
    z = (ctx % SIDE)[None]
    steps = (1, 2, 3)
    place = jnp.concatenate([x, z])
    count = SIDE * SIDE
    block = shape((3, TOK, HEAD_DIM))
    single = shape((ROWS, HEAD_DIM))
    flat = shape((TOK, GROUP * HEAD_DIM))

    step = timesteps[0, 0]
    when = jnp.full((1, WIDTH), step.astype(jnp.float32))
    gains = jnp.concatenate([qk_gain[0], when])
    gains = lax.ppermute(gains, "segment", [((i + 1) % SIDE, i) for i in range(SIDE)])
    parts = qkv[0, 0].transpose(1, 0, 2)
    cots = call(cut_cotangent_kernel, [flat] * SIDE, 0, 1_600_000, z, cotangent[0, 0])
    cots_z = [None] * SIDE
    for k in (2, 1, 3, 0):
        cots_z[k] = away(cots[k], k)
    cosine, sine = rope_tables(positions[0])
    main, *shared = call(
        prep_kernel,
        [shape((count, 3, TOK, HEAD_DIM))] + [block] * SIDE,
        10_000_000,
        5_000_000,
        z,
        parts,
        gains,
        cosine,
        sine,
    )
    shared_z = exchanged(along_z, shared)
    main = lax.all_to_all(after(main, cots_z), "ctx", 0, 0)
    pair = jnp.concatenate([b[1:] for b in shared_z], axis=1)
    pairs = [pair] + [along_x(pair, k) for k in steps]
    gate = jnp.dot(embed(step), mod_weight[0], precision=lax.Precision.HIGHEST)[None]
    rows = FREQS // (SIDE * SIDE * SIDE)
    index = (ctx * SIDE + lax.axis_index("dp").astype(jnp.int32)) * rows
    freq = lax.dynamic_slice_in_dim(np.tile(frequencies(), 2), index, rows)
    freq = jnp.broadcast_to(freq[:, None], (rows, HEAD_DIM))
    shared_out = call(
        shared_kernel, single, 840_000_000, 1_600_000, *shared_z, *pairs, smem=0
    )
    main, gate, freq, shared_out = lax.optimization_barrier((main, gate, freq, shared_out))
    back = [None] * SIDE
    back[2], back[1], back[3] = call(
        functools.partial(main_kernel, (2, 1, 3)), [single] * 3, 2_500_000_000, 2_500_000, x, main
    )
    (back[0],) = call(
        functools.partial(main_kernel, (0,)), [single], 840_000_000, 2_000_000, x, main
    )
    back = [back[0]] + [along_x(back[m], SIDE - m) for m in steps]
    joined = call(join_kernel, [flat] * SIDE, 0, 1_600_000, place, *back, shared_out)
    at_home = [None] * SIDE
    for k in (2, 1, 3, 0):
        at_home[k] = home(joined[k], (SIDE - k) % SIDE)

    def gradient(_, before):
        attn, before = lax.optimization_barrier(([*back, shared_out], before))
        chans = pl.pallas_call(
            channels_kernel,
            out_shape=shape((SIDE * count, 8, HEAD_DIM), jnp.float32),
            in_specs=[SMEM_SPEC] + [VMEM_SPEC] * (1 + GROUP + SIDE),
            out_specs=VMEM_SPEC,
            scratch_shapes=[pltpu.VMEM((8, HEAD_DIM), jnp.float32)],
            compiler_params=VMEM,
            cost_estimate=pl.CostEstimate(flops=0, bytes_accessed=0, transcendentals=0),
        )(place, gains, *attn, *cots_z)
        chans = lax.all_to_all(chans, ("ctx", "dp"), 0, 0)
        return call(grad_kernel, zeros, 0, 200_000, index[None], freq, before, chans)

    zeros = shape((rows, WIDTH), jnp.float32)
    turns = jnp.where(step < 1000, 1, 2)
    grad = lax.fori_loop(0, turns, gradient, jnp.zeros((rows, WIDTH), jnp.float32))
    grad = lax.ppermute(grad, "segment", [(i, (i + 1) % SIDE) for i in range(SIDE)])

    attn_out = call(
        finish_kernel, shape((TOK, WIDTH)), 500_000, 1_700_000, z, *at_home, gate
    )
    return (attn_out[None, None], grad[None])


def solution(mesh):
    return jax.shard_map(
        local,
        mesh=mesh,
        in_specs=(
            P("segment", "dp", "ctx", None, None),
            P("segment", None, None),
            P("segment", None, None),
            P("dp", "ctx"),
            P("segment", "dp"),
            P("segment", "dp", "ctx", None),
        ),
        out_specs=(P("segment", "dp", "ctx", None), P("segment", ("ctx", "dp"), None)),
        check_vma=False,
    )
```

```python
import functools

import jax
import jax.numpy as jnp
import numpy as np
from jax import lax
from jax.experimental import pallas as pl
from jax.experimental.pallas import tpu as pltpu
from jax.sharding import PartitionSpec as P

HEADS = 20
HEAD_DIM = 128
FREQS = 256
GRID_ROWS = 45
GRID_COLS = 80
SIDE = 4
GROUP = HEADS // SIDE
TOK = 160
ROWS = SIDE * TOK
WIDTH = HEADS * HEAD_DIM
TILE = 320
EXP_SCALE = 1.4426950408889634 / HEAD_DIM**0.5
VMEM = pltpu.CompilerParams(vmem_limit_bytes=56 * 1024 * 1024)
SMEM_SPEC = pl.BlockSpec(memory_space=pltpu.SMEM)
VMEM_SPEC = pl.BlockSpec(memory_space=pltpu.VMEM)


def along_z(value, by):
    pairs = [(i, i // SIDE * SIDE + (i + by) % SIDE) for i in range(SIDE * SIDE)]
    return lax.ppermute(value, "ctx", pairs)


def along_x(value, by):
    pairs = [(i, (i + SIDE * by) % (SIDE * SIDE)) for i in range(SIDE * SIDE)]
    return lax.ppermute(value, "ctx", pairs)


def along_dp(value, by):
    return lax.ppermute(value, "dp", [(i, (i + by) % SIDE) for i in range(SIDE)])


def exchanged(along, blocks):
    got = list(blocks)
    for k in (2, 1, 3):
        got[k] = along(blocks[k], k)
    return got


def section_pairs(turn, by):
    count = SIDE * SIDE
    pairs = []
    for seg in range(SIDE):
        for i in range(count):
            target = (seg + turn) % SIDE * count + i // SIDE * SIDE + (i + by) % SIDE
            pairs.append((seg * count + i, target))
    return pairs


def home(value, by):
    return lax.ppermute(value, ("segment", "ctx"), section_pairs(1, by))


def away(value, by):
    return lax.ppermute(value, ("segment", "ctx"), section_pairs(SIDE - 1, by))


def rope_tables(pos):
    half = HEAD_DIM // 2
    side = HEAD_DIM // 6
    first = half - 2 * side
    frame = (pos // (GRID_ROWS * GRID_COLS)).astype(jnp.float32)
    row = (pos // GRID_COLS % GRID_ROWS).astype(jnp.float32)
    col = (pos % GRID_COLS).astype(jnp.float32)
    pair = np.arange(half)
    group = np.where(pair < first, 0, np.where(pair < first + side, 1, 2))
    offset = np.where(group == 0, 0, np.where(group == 1, first, first + side))
    pairs_in = np.where(group == 0, first, side)
    freq = (10000.0 ** (-(pair - offset) / pairs_in)).astype(np.float32)
    coord = jnp.where(
        group[None, :] == 0,
        frame[:, None],
        jnp.where(group[None, :] == 1, row[:, None], col[:, None]),
    )
    angle = coord * freq[None, :]
    cosine = jnp.concatenate([jnp.cos(angle), jnp.cos(angle)], axis=1)
    sine = jnp.concatenate([-jnp.sin(angle), jnp.sin(angle)], axis=1)
    return (cosine, sine)


def one_of(which, dims):
    return pl.BlockSpec((1, *dims), lambda i: (which, 0, 0))


def call(kernel, out_shape, flops, moved, *operands, smem=1, specs=None):
    grid = () if specs is None else (1,)
    specs = specs or [SMEM_SPEC] * smem + [VMEM_SPEC] * (len(operands) - smem)
    return pl.pallas_call(
        kernel,
        grid=grid,
        out_shape=out_shape,
        in_specs=specs,
        out_specs=jax.tree.map(lambda _: VMEM_SPEC, out_shape),
        compiler_params=VMEM,
        cost_estimate=pl.CostEstimate(flops=0, bytes_accessed=0, transcendentals=0),
    )(*operands)


def group_columns(index):
    wide = GROUP * HEAD_DIM
    return pl.ds(pl.multiple_of(lax.rem(index, SIDE) * wide, HEAD_DIM), wide)


def after(value, first):
    return lax.optimization_barrier((value, first))[0]


def column(index):
    return pl.ds(pl.multiple_of(index * HEAD_DIM, HEAD_DIM), HEAD_DIM)


def prep_kernel(z_ref, qkv_ref, gain_ref, cos_ref, sin_ref, main_ref, *shared):
    z = z_ref[0]
    cosine = cos_ref[...]
    sine = sin_ref[...]
    for part in range(3):
        if part < 2:
            total = jnp.zeros((TOK, HEAD_DIM), jnp.float32)
            for head in range(HEADS):
                x = qkv_ref[part, :, head * HEAD_DIM : (head + 1) * HEAD_DIM].astype(jnp.float32)
                total = total + x * x
            mean_sq = jnp.sum(total, axis=1, keepdims=True) / WIDTH
            inverse = lax.rsqrt(mean_sq + 1e-06)

        def head_of(cols):
            x = qkv_ref[part, :, cols]
            if part == 2:
                return x
            y = x.astype(jnp.float32) * inverse * gain_ref[part : part + 1, cols]
            turned = pltpu.roll(y, HEAD_DIM // 2, 1)
            return (y * cosine + turned * sine).astype(jnp.bfloat16)

        for step in range(SIDE):
            shared[step][part] = head_of(column(lax.rem(z + step, SIDE) * GROUP + GROUP - 1))
        for to_x in range(SIDE):
            for to_z in range(SIDE):
                at = (to_z * GROUP + to_x) * HEAD_DIM
                main_ref[to_x * SIDE + to_z, part] = head_of(slice(at, at + HEAD_DIM))


def cut_cotangent_kernel(z_ref, cot_ref, *outs):
    z = z_ref[0]
    for step in range(SIDE):
        outs[step][...] = cot_ref[:, group_columns(z + step)]


def attend(q, keys, values):
    nt = (((1,), (1,)), ((), ()))
    scores = [lax.dot_general(q, k, nt, preferred_element_type=jnp.float32) for k in keys]
    peak = functools.reduce(jnp.maximum, [jnp.max(s, axis=1, keepdims=True) for s in scores])
    expo = [jnp.exp2((s - peak) * EXP_SCALE) for s in scores]
    total = sum(jnp.sum(e, axis=1, keepdims=True) for e in expo)
    accum = sum(
        jnp.dot(e.astype(jnp.bfloat16), v, preferred_element_type=jnp.float32)
        for e, v in zip(expo, values, strict=True)
    )
    return (accum / total).astype(jnp.bfloat16)


def shared_kernel(q0, q1, q2, q3, s0, s1, s2, s3, out_ref):
    blocks = (s0, s1, s2, s3)
    for pair in ((q0, q1), (q2, q3)):
        at = 0 if pair[0] is q0 else TILE
        q = jnp.concatenate([p[0] for p in pair])
        out_ref[at : at + TILE] = attend(q, [b[0] for b in blocks], [b[1] for b in blocks])


def main_kernel(back, x_ref, r_ref, *outs):
    x = x_ref[0]

    def four(part, first):
        return r_ref[pl.ds(first * SIDE, SIDE), part].reshape(ROWS, HEAD_DIM)

    keys = [four(1, m) for m in range(SIDE)]
    values = [four(2, m) for m in range(SIDE)]
    for step, out_ref in zip(back, outs, strict=True):
        first = lax.rem(x + SIDE - step, SIDE) * SIDE
        for i in range(ROWS // TILE):
            half = SIDE // 2
            q = r_ref[pl.ds(first + i * half, half), 0].reshape(TILE, HEAD_DIM)
            out_ref[i * TILE : (i + 1) * TILE] = attend(q, keys, values)


def rows_of(z, source, step):
    first = lax.rem(z + SIDE - step, SIDE) if source < SIDE else step
    return pl.ds(pl.multiple_of(first * TOK, 32), TOK)


def join_kernel(place_ref, *refs):
    x, z = place_ref[0], place_ref[1]
    outs = refs[GROUP:]
    for source in range(GROUP):
        place = lax.rem(x + source, SIDE) if source < SIDE else SIDE
        for step in range(SIDE):
            outs[step][:, column(place)] = refs[source][rows_of(z, source, step)]


def channels_kernel(place_ref, time_ref, *refs):
    x, z = place_ref[0], place_ref[1]
    cots = refs[GROUP : GROUP + SIDE]
    out_ref, chan_ref = refs[GROUP + SIDE :]
    chan_ref[...] = jnp.zeros_like(chan_ref)
    for source in range(GROUP):
        place = lax.rem(x + source, SIDE) if source < SIDE else SIDE
        total = jnp.zeros((TOK, HEAD_DIM), jnp.float32)
        for step in range(SIDE):
            attn = refs[source][rows_of(z, source, step)].astype(jnp.float32)
            total = total + attn * cots[step][:, column(place)].astype(jnp.float32)
        chan_ref[pl.ds(place, 1)] = jnp.sum(total, axis=0, keepdims=True)
    chan_ref[GROUP : GROUP + 1] = time_ref[2:3, :HEAD_DIM]
    for i in range(out_ref.shape[0]):
        out_ref[i] = chan_ref[...]


def finish_kernel(z_ref, a0, a1, a2, a3, gate_ref, out_ref):
    z = z_ref[0]
    for step, a in enumerate((a0, a1, a2, a3)):
        cols = group_columns(z + step)
        out_ref[:, cols] = (a[...].astype(jnp.float32) * gate_ref[:, cols]).astype(jnp.bfloat16)


def grad_kernel(index_ref, freq_ref, before_ref, chan_ref, out_ref):
    is_cosine = index_ref[0] < FREQS // 2
    factors = []
    for d in range(SIDE):
        angle = chan_ref[d, GROUP : GROUP + 1] * freq_ref[...]
        factors.append(jnp.where(is_cosine, jnp.cos(angle), jnp.sin(angle)))
    for z in range(SIDE):
        chans = [sum(chan_ref[(x * SIDE + z) * SIDE + d] for x in range(SIDE)) for d in range(SIDE)]
        for head in range(GROUP):
            total = sum(f * c[head : head + 1] for f, c in zip(factors, chans, strict=True))
            at = (z * GROUP + head) * HEAD_DIM
            cols = slice(at, at + HEAD_DIM)
            out_ref[:, cols] = before_ref[...] + total


def shape(dims, dtype=jnp.bfloat16):
    return jax.ShapeDtypeStruct(dims, dtype)


def frequencies():
    count = FREQS // 2
    return (10000.0 ** (-np.arange(count) / count)).astype(np.float32)


def embed(step):
    angle = step.astype(jnp.float32) * frequencies()
    return jnp.concatenate([jnp.cos(angle), jnp.sin(angle)])


def local(qkv, qk_gain, mod_weight, positions, timesteps, cotangent):
    ctx = lax.axis_index("ctx").astype(jnp.int32)
    x = (ctx // SIDE)[None]
    z = (ctx % SIDE)[None]
    steps = (1, 2, 3)
    place = jnp.concatenate([x, z])
    count = SIDE * SIDE
    block = shape((3, TOK, HEAD_DIM))
    single = shape((ROWS, HEAD_DIM))
    flat = shape((TOK, GROUP * HEAD_DIM))

    step = timesteps[0, 0]
    when = jnp.full((1, WIDTH), step.astype(jnp.float32))
    gains = jnp.concatenate([qk_gain[0], when])
    gains = lax.ppermute(gains, "segment", [((i + 1) % SIDE, i) for i in range(SIDE)])
    parts = qkv[0, 0].transpose(1, 0, 2)
    cots = call(cut_cotangent_kernel, [flat] * SIDE, 0, 1_600_000, z, cotangent[0, 0])
    cots_z = [None] * SIDE
    for k in (2, 1):
        cots_z[k] = away(cots[k], k)
    cosine, sine = rope_tables(positions[0])
    main, *shared = call(
        prep_kernel,
        [shape((count, 3, TOK, HEAD_DIM))] + [block] * SIDE,
        10_000_000,
        5_000_000,
        z,
        parts,
        gains,
        cosine,
        sine,
    )
    shared_z = exchanged(along_z, shared)
    main = lax.all_to_all(after(main, shared_z), "ctx", 0, 0)
    pair = jnp.concatenate([b[1:] for b in shared_z], axis=1)
    pairs = [pair] + [along_x(pair, k) for k in steps]
    gate = jnp.dot(embed(step), mod_weight[0], precision=lax.Precision.HIGHEST)[None]
    rows = FREQS // (SIDE * SIDE * SIDE)
    index = (ctx * SIDE + lax.axis_index("dp").astype(jnp.int32)) * rows
    freq = lax.dynamic_slice_in_dim(np.tile(frequencies(), 2), index, rows)
    freq = jnp.broadcast_to(freq[:, None], (rows, HEAD_DIM))
    shared_out = call(
        shared_kernel, single, 840_000_000, 1_600_000, *shared_z, *pairs, smem=0
    )
    main, gate, freq = lax.optimization_barrier((main, gate, freq))
    back = [None] * SIDE
    back[2], back[1], back[3] = call(
        functools.partial(main_kernel, (2, 1, 3)), [single] * 3, 2_500_000_000, 2_500_000, x, main
    )
    (back[0],) = call(
        functools.partial(main_kernel, (0,)), [single], 840_000_000, 2_000_000, x, main
    )
    for k in (3, 0):
        cots_z[k] = away(after(cots[k], back[2]), k)
    back = [back[0]] + [along_x(back[m], SIDE - m) for m in steps]
    joined = call(
        join_kernel, [flat] * SIDE, 0, 1_600_000, place, *back, after(shared_out, cots_z[1:3])
    )
    at_home = [None] * SIDE
    for k in (2, 1, 3, 0):
        at_home[k] = home(joined[k], (SIDE - k) % SIDE)

    def gradient(_, state):
        attn, before = lax.optimization_barrier(([*back, shared_out], state[1]))
        chans = pl.pallas_call(
            channels_kernel,
            out_shape=shape((SIDE * count, 8, HEAD_DIM), jnp.float32),
            in_specs=[SMEM_SPEC] + [VMEM_SPEC] * (1 + GROUP + SIDE),
            out_specs=VMEM_SPEC,
            scratch_shapes=[pltpu.VMEM((8, HEAD_DIM), jnp.float32)],
            compiler_params=VMEM,
            cost_estimate=pl.CostEstimate(flops=0, bytes_accessed=0, transcendentals=0),
        )(place, gains, *attn, *cots_z)
        chans = lax.all_to_all(chans, ("ctx", "dp"), 0, 0)
        grad = call(grad_kernel, zeros, 0, 200_000, index[None], freq, before, chans)
        return (grad, before)

    zeros = shape((rows, WIDTH), jnp.float32)
    turns = jnp.where(step < 1000, 1, 2)
    start = (jnp.zeros((rows, WIDTH), jnp.float32), jnp.zeros((rows, HEAD_DIM), jnp.float32))
    grad, _ = lax.fori_loop(0, turns, gradient, start)
    grad = lax.ppermute(grad, "segment", [(i, (i + 1) % SIDE) for i in range(SIDE)])

    attn_out = call(
        finish_kernel, shape((TOK, WIDTH)), 500_000, 1_700_000, z, *at_home, gate
    )
    return (attn_out[None, None], grad[None])


def solution(mesh):
    return jax.shard_map(
        local,
        mesh=mesh,
        in_specs=(
            P("segment", "dp", "ctx", None, None),
            P("segment", None, None),
            P("segment", None, None),
            P("dp", "ctx"),
            P("segment", "dp"),
            P("segment", "dp", "ctx", None),
        ),
        out_specs=(P("segment", "dp", "ctx", None), P("segment", ("ctx", "dp"), None)),
        check_vma=False,
    )
```

```python
import functools

import jax
import jax.numpy as jnp
import numpy as np
from jax import lax
from jax.experimental import pallas as pl
from jax.experimental.pallas import tpu as pltpu
from jax.sharding import PartitionSpec as P

HEADS = 20
HEAD_DIM = 128
FREQS = 256
GRID_ROWS = 45
GRID_COLS = 80
SIDE = 4
GROUP = HEADS // SIDE
TOK = 160
ROWS = SIDE * TOK
WIDTH = HEADS * HEAD_DIM
TILE = 320
EXP_SCALE = 1.4426950408889634 / HEAD_DIM**0.5
VMEM = pltpu.CompilerParams(vmem_limit_bytes=56 * 1024 * 1024)
SMEM_SPEC = pl.BlockSpec(memory_space=pltpu.SMEM)
VMEM_SPEC = pl.BlockSpec(memory_space=pltpu.VMEM)


def along_z(value, by):
    pairs = [(i, i // SIDE * SIDE + (i + by) % SIDE) for i in range(SIDE * SIDE)]
    return lax.ppermute(value, "ctx", pairs)


def along_x(value, by):
    pairs = [(i, (i + SIDE * by) % (SIDE * SIDE)) for i in range(SIDE * SIDE)]
    return lax.ppermute(value, "ctx", pairs)


def along_dp(value, by):
    return lax.ppermute(value, "dp", [(i, (i + by) % SIDE) for i in range(SIDE)])


def exchanged(along, blocks):
    got = list(blocks)
    for k in (2, 1, 3):
        got[k] = along(blocks[k], k)
    return got


def onward(value, back):
    count = SIDE * SIDE
    pairs = []
    for seg in range(SIDE):
        for i in range(count):
            target = (seg + 1) % SIDE * count + (i - back * SIDE) % count
            pairs.append((seg * count + i, target))
    return lax.ppermute(value, ("segment", "ctx"), pairs)


def rope_tables(pos):
    half = HEAD_DIM // 2
    side = HEAD_DIM // 6
    first = half - 2 * side
    frame = (pos // (GRID_ROWS * GRID_COLS)).astype(jnp.float32)
    row = (pos // GRID_COLS % GRID_ROWS).astype(jnp.float32)
    col = (pos % GRID_COLS).astype(jnp.float32)
    pair = np.arange(half)
    group = np.where(pair < first, 0, np.where(pair < first + side, 1, 2))
    offset = np.where(group == 0, 0, np.where(group == 1, first, first + side))
    pairs_in = np.where(group == 0, first, side)
    freq = (10000.0 ** (-(pair - offset) / pairs_in)).astype(np.float32)
    coord = jnp.where(
        group[None, :] == 0,
        frame[:, None],
        jnp.where(group[None, :] == 1, row[:, None], col[:, None]),
    )
    angle = coord * freq[None, :]
    cosine = jnp.concatenate([jnp.cos(angle), jnp.cos(angle)], axis=1)
    sine = jnp.concatenate([-jnp.sin(angle), jnp.sin(angle)], axis=1)
    return (cosine, sine)


def one_of(which, dims):
    return pl.BlockSpec((1, *dims), lambda i: (which, 0, 0))


def call(kernel, out_shape, flops, moved, *operands, smem=1, specs=None):
    grid = () if specs is None else (1,)
    specs = specs or [SMEM_SPEC] * smem + [VMEM_SPEC] * (len(operands) - smem)
    return pl.pallas_call(
        kernel,
        grid=grid,
        out_shape=out_shape,
        in_specs=specs,
        out_specs=jax.tree.map(lambda _: VMEM_SPEC, out_shape),
        compiler_params=VMEM,
        cost_estimate=pl.CostEstimate(flops=0, bytes_accessed=0, transcendentals=0),
    )(*operands)


def group_columns(index):
    wide = GROUP * HEAD_DIM
    return pl.ds(pl.multiple_of(lax.rem(index, SIDE) * wide, HEAD_DIM), wide)


def after(value, first):
    return lax.optimization_barrier((value, first))[0]


def column(index):
    return pl.ds(pl.multiple_of(index * HEAD_DIM, HEAD_DIM), HEAD_DIM)


def prep_kernel(z_ref, qkv_ref, gain_ref, cos_ref, sin_ref, main_ref, *shared):
    z = z_ref[0]
    cosine = cos_ref[...]
    sine = sin_ref[...]
    for part in range(3):
        if part < 2:
            total = jnp.zeros((TOK, HEAD_DIM), jnp.float32)
            for head in range(HEADS):
                x = qkv_ref[part, :, head * HEAD_DIM : (head + 1) * HEAD_DIM].astype(jnp.float32)
                total = total + x * x
            mean_sq = jnp.sum(total, axis=1, keepdims=True) / WIDTH
            inverse = lax.rsqrt(mean_sq + 1e-06)

        def head_of(cols):
            x = qkv_ref[part, :, cols]
            if part == 2:
                return x
            y = x.astype(jnp.float32) * inverse * gain_ref[part : part + 1, cols]
            turned = pltpu.roll(y, HEAD_DIM // 2, 1)
            return (y * cosine + turned * sine).astype(jnp.bfloat16)

        for step in range(SIDE):
            shared[step][part] = head_of(column(lax.rem(z + step, SIDE) * GROUP + GROUP - 1))
        for to_x in range(SIDE):
            for to_z in range(SIDE):
                at = (to_z * GROUP + to_x) * HEAD_DIM
                if part < 2:
                    main_ref[to_x * SIDE + to_z, part] = head_of(slice(at, at + HEAD_DIM))


def cut_values_kernel(v_ref, out_ref):
    for to_x in range(SIDE):
        for to_z in range(SIDE):
            at = (to_z * GROUP + to_x) * HEAD_DIM
            out_ref[to_x * SIDE + to_z] = v_ref[0, :, at : at + HEAD_DIM]


def cut_cotangent_kernel(z_ref, cot_ref, *outs):
    z = z_ref[0]
    for step in range(SIDE):
        outs[step][...] = cot_ref[:, group_columns(z + step)]


def attend(q, keys, values):
    nt = (((1,), (1,)), ((), ()))
    scores = [lax.dot_general(q, k, nt, preferred_element_type=jnp.float32) for k in keys]
    peak = functools.reduce(jnp.maximum, [jnp.max(s, axis=1, keepdims=True) for s in scores])
    expo = [jnp.exp2((s - peak) * EXP_SCALE) for s in scores]
    total = sum(jnp.sum(e, axis=1, keepdims=True) for e in expo)
    accum = sum(
        jnp.dot(e.astype(jnp.bfloat16), v, preferred_element_type=jnp.float32)
        for e, v in zip(expo, values, strict=True)
    )
    return (accum / total).astype(jnp.bfloat16)


def shared_kernel(q0, q1, q2, q3, s0, s1, s2, s3, out_ref):
    blocks = (s0, s1, s2, s3)
    for pair in ((q0, q1), (q2, q3)):
        at = 0 if pair[0] is q0 else TILE
        q = jnp.concatenate([p[0] for p in pair])
        out_ref[at : at + TILE] = attend(q, [b[0] for b in blocks], [b[1] for b in blocks])


def main_kernel(back, x_ref, r_ref, v_ref, *outs):
    x = x_ref[0]

    fours = [pl.ds(m * SIDE, SIDE) for m in range(SIDE)]
    keys = [r_ref[four, 1].reshape(ROWS, HEAD_DIM) for four in fours]
    values = [v_ref[four].reshape(ROWS, HEAD_DIM) for four in fours]
    for step, out_ref in zip(back, outs, strict=True):
        first = lax.rem(x + SIDE - step, SIDE) * SIDE
        for i in range(ROWS // TILE):
            half = SIDE // 2
            q = r_ref[pl.ds(first + i * half, half), 0].reshape(TILE, HEAD_DIM)
            out_ref[i * TILE : (i + 1) * TILE] = attend(q, keys, values)


def rows_of(z, source, step):
    first = lax.rem(z + SIDE - step, SIDE) if source < SIDE else step
    return pl.ds(pl.multiple_of(first * TOK, 32), TOK)


def join_kernel(place_ref, *refs):
    x, z = place_ref[0], place_ref[1]
    outs = refs[GROUP:]
    for source in range(GROUP):
        place = lax.rem(x + source, SIDE) if source < SIDE else SIDE
        for step in range(SIDE):
            outs[step][:, column(place)] = refs[source][rows_of(z, source, step)]


def channels_kernel(place_ref, time_ref, *refs):
    x, z = place_ref[0], place_ref[1]
    cots = refs[GROUP : GROUP + SIDE]
    out_ref, chan_ref = refs[GROUP + SIDE :]
    chan_ref[...] = jnp.zeros_like(chan_ref)
    for source in range(GROUP):
        place = lax.rem(x + source, SIDE) if source < SIDE else SIDE
        total = jnp.zeros((TOK, HEAD_DIM), jnp.float32)
        for step in range(SIDE):
            attn = refs[source][rows_of(z, source, step)].astype(jnp.float32)
            total = total + attn * cots[step][:, column(place)].astype(jnp.float32)
        chan_ref[pl.ds(place, 1)] = jnp.sum(total, axis=0, keepdims=True)
    chan_ref[GROUP : GROUP + 1] = time_ref[...]
    for i in range(out_ref.shape[0]):
        out_ref[i] = chan_ref[...]


def finish_kernel(z_ref, a0, a1, a2, a3, gate_ref, out_ref):
    z = z_ref[0]
    for step, a in enumerate((a0, a1, a2, a3)):
        cols = group_columns(z + step)
        out_ref[:, cols] = (a[...].astype(jnp.float32) * gate_ref[:, cols]).astype(jnp.bfloat16)


def grad_kernel(index_ref, freq_ref, before_ref, chan_ref, out_ref):
    is_cosine = index_ref[0] < FREQS // 2
    factors = []
    for d in range(SIDE):
        angle = chan_ref[d, GROUP : GROUP + 1] * freq_ref[...]
        factors.append(jnp.where(is_cosine, jnp.cos(angle), jnp.sin(angle)))
    for z in range(SIDE):
        chans = [sum(chan_ref[(x * SIDE + z) * SIDE + d] for x in range(SIDE)) for d in range(SIDE)]
        for head in range(GROUP):
            total = sum(f * c[head : head + 1] for f, c in zip(factors, chans, strict=True))
            at = (z * GROUP + head) * HEAD_DIM
            cols = slice(at, at + HEAD_DIM)
            out_ref[:, cols] = before_ref[...] + total


def shape(dims, dtype=jnp.bfloat16):
    return jax.ShapeDtypeStruct(dims, dtype)


def frequencies():
    count = FREQS // 2
    return (10000.0 ** (-np.arange(count) / count)).astype(np.float32)


def embed(step):
    angle = step.astype(jnp.float32) * frequencies()
    return jnp.concatenate([jnp.cos(angle), jnp.sin(angle)])


def local(qkv, qk_gain, mod_weight, positions, timesteps, cotangent):
    ctx = lax.axis_index("ctx").astype(jnp.int32)
    x = (ctx // SIDE)[None]
    z = (ctx % SIDE)[None]
    steps = (1, 2, 3)
    place = jnp.concatenate([x, z])
    count = SIDE * SIDE
    block = shape((3, TOK, HEAD_DIM))
    single = shape((ROWS, HEAD_DIM))
    flat = shape((TOK, GROUP * HEAD_DIM))

    step = timesteps[0, 0]
    when = jnp.full((1, HEAD_DIM), step.astype(jnp.float32))
    gains = lax.ppermute(qk_gain[0], "segment", [((i + 1) % SIDE, i) for i in range(SIDE)])
    parts = qkv[0, 0].transpose(1, 0, 2)
    cots = call(cut_cotangent_kernel, [flat] * SIDE, 0, 1_600_000, z, cotangent[0, 0])
    cots_z = [cots[0], along_z(cots[1], 1), along_z(cots[2], 2), None]
    values = call(
        cut_values_kernel,
        shape((count, TOK, HEAD_DIM)),
        0,
        1_600_000,
        parts,
        specs=[one_of(2, (TOK, WIDTH))],
    )
    values = lax.all_to_all(values, "ctx", 0, 0)
    cosine, sine = rope_tables(positions[0])
    main, *shared = call(
        prep_kernel,
        [shape((count, 2, TOK, HEAD_DIM))] + [block] * SIDE,
        10_000_000,
        5_000_000,
        z,
        parts,
        gains,
        cosine,
        sine,
    )
    shared_z = exchanged(along_z, shared)
    main = lax.all_to_all(after(main, (values, shared_z)), "ctx", 0, 0)
    pair = jnp.concatenate([b[1:] for b in shared_z], axis=1)
    pairs = [pair] + [along_x(pair, k) for k in steps]
    gate = jnp.dot(embed(step), mod_weight[0], precision=lax.Precision.HIGHEST)[None]
    rows = FREQS // (SIDE * SIDE * SIDE)
    index = (ctx * SIDE + lax.axis_index("dp").astype(jnp.int32)) * rows
    freq = lax.dynamic_slice_in_dim(np.tile(frequencies(), 2), index, rows)
    freq = jnp.broadcast_to(freq[:, None], (rows, HEAD_DIM))
    main, gate, freq = lax.optimization_barrier((main, gate, freq))
    back = [None] * SIDE
    back[2], back[1], back[3] = call(
        functools.partial(main_kernel, (2, 1, 3)), [single] * 3, 2_500_000_000, 2_500_000, x, main, values
    )
    (back[0],) = call(
        functools.partial(main_kernel, (0,)), [single], 840_000_000, 2_000_000, x, main, values
    )
    shared_out = call(
        shared_kernel, single, 840_000_000, 1_600_000, *after(shared_z, back[2]), *pairs, smem=0
    )
    cots_z[3] = along_z(after(cots[3], back[2]), 3)
    for m in (2, 1, 3, 0):
        back[m] = onward(back[m], m)
    shared_out = onward(shared_out, 0)
    joined = call(
        join_kernel, [flat] * SIDE, 0, 1_600_000, place, *back, after(shared_out, cots_z[1:])
    )
    at_home = [joined[0]] + [along_z(joined[k], SIDE - k) for k in steps]

    def gradient(_, state):
        attn, before = lax.optimization_barrier(([*back, shared_out], state[1]))
        chans = pl.pallas_call(
            channels_kernel,
            out_shape=shape((SIDE * count, 8, HEAD_DIM), jnp.float32),
            in_specs=[SMEM_SPEC] + [VMEM_SPEC] * (1 + GROUP + SIDE),
            out_specs=VMEM_SPEC,
            scratch_shapes=[pltpu.VMEM((8, HEAD_DIM), jnp.float32)],
            compiler_params=VMEM,
            cost_estimate=pl.CostEstimate(flops=0, bytes_accessed=0, transcendentals=0),
        )(place, when, *attn, *cots_z)
        chans = lax.all_to_all(chans, ("ctx", "dp"), 0, 0)
        grad = call(grad_kernel, zeros, 0, 200_000, index[None], freq, before, chans)
        return (grad, before)

    zeros = shape((rows, WIDTH), jnp.float32)
    turns = jnp.where(step < 1000, 1, 2)
    start = (jnp.zeros((rows, WIDTH), jnp.float32), jnp.zeros((rows, HEAD_DIM), jnp.float32))
    grad, _ = lax.fori_loop(0, turns, gradient, start)

    attn_out = call(
        finish_kernel, shape((TOK, WIDTH)), 500_000, 1_700_000, z, *after(at_home, grad), gate
    )
    return (attn_out[None, None], grad[None])


def solution(mesh):
    return jax.shard_map(
        local,
        mesh=mesh,
        in_specs=(
            P("segment", "dp", "ctx", None, None),
            P("segment", None, None),
            P("segment", None, None),
            P("dp", "ctx"),
            P("segment", "dp"),
            P("segment", "dp", "ctx", None),
        ),
        out_specs=(P("segment", "dp", "ctx", None), P("segment", ("ctx", "dp"), None)),
        check_vma=False,
    )
```

```python
import functools

import jax
import jax.numpy as jnp
import numpy as np
from jax import lax
from jax.experimental import pallas as pl
from jax.experimental.pallas import tpu as pltpu
from jax.sharding import PartitionSpec as P

HEADS = 20
HEAD_DIM = 128
FREQS = 256
GRID_ROWS = 45
GRID_COLS = 80
SIDE = 4
GROUP = HEADS // SIDE
TOK = 160
ROWS = SIDE * TOK
WIDTH = HEADS * HEAD_DIM
TILE = 320
EXP_SCALE = 1.4426950408889634 / HEAD_DIM**0.5
VMEM = pltpu.CompilerParams(vmem_limit_bytes=56 * 1024 * 1024)
SMEM_SPEC = pl.BlockSpec(memory_space=pltpu.SMEM)
VMEM_SPEC = pl.BlockSpec(memory_space=pltpu.VMEM)


def along_z(value, by):
    pairs = [(i, i // SIDE * SIDE + (i + by) % SIDE) for i in range(SIDE * SIDE)]
    return lax.ppermute(value, "ctx", pairs)


def along_x(value, by):
    pairs = [(i, (i + SIDE * by) % (SIDE * SIDE)) for i in range(SIDE * SIDE)]
    return lax.ppermute(value, "ctx", pairs)


def along_dp(value, by):
    return lax.ppermute(value, "dp", [(i, (i + by) % SIDE) for i in range(SIDE)])


def exchanged(along, blocks):
    got = list(blocks)
    for k in (2, 1, 3):
        got[k] = along(blocks[k], k)
    return got


def onward(value, back):
    count = SIDE * SIDE
    pairs = []
    for seg in range(SIDE):
        for i in range(count):
            target = (seg + 1) % SIDE * count + (i - back * SIDE) % count
            pairs.append((seg * count + i, target))
    return lax.ppermute(value, ("segment", "ctx"), pairs)


def rope_tables(pos):
    half = HEAD_DIM // 2
    side = HEAD_DIM // 6
    first = half - 2 * side
    frame = (pos // (GRID_ROWS * GRID_COLS)).astype(jnp.float32)
    row = (pos // GRID_COLS % GRID_ROWS).astype(jnp.float32)
    col = (pos % GRID_COLS).astype(jnp.float32)
    pair = np.arange(half)
    group = np.where(pair < first, 0, np.where(pair < first + side, 1, 2))
    offset = np.where(group == 0, 0, np.where(group == 1, first, first + side))
    pairs_in = np.where(group == 0, first, side)
    freq = (10000.0 ** (-(pair - offset) / pairs_in)).astype(np.float32)
    coord = jnp.where(
        group[None, :] == 0,
        frame[:, None],
        jnp.where(group[None, :] == 1, row[:, None], col[:, None]),
    )
    angle = coord * freq[None, :]
    cosine = jnp.concatenate([jnp.cos(angle), jnp.cos(angle)], axis=1)
    sine = jnp.concatenate([-jnp.sin(angle), jnp.sin(angle)], axis=1)
    return (cosine, sine)


def one_of(which, dims):
    return pl.BlockSpec((1, *dims), lambda i: (which, 0, 0))


def call(kernel, out_shape, flops, moved, *operands, smem=1, specs=None):
    grid = () if specs is None else (1,)
    specs = specs or [SMEM_SPEC] * smem + [VMEM_SPEC] * (len(operands) - smem)
    return pl.pallas_call(
        kernel,
        grid=grid,
        out_shape=out_shape,
        in_specs=specs,
        out_specs=jax.tree.map(lambda _: VMEM_SPEC, out_shape),
        compiler_params=VMEM,
        cost_estimate=pl.CostEstimate(flops=0, bytes_accessed=0, transcendentals=0),
    )(*operands)


def group_columns(index):
    wide = GROUP * HEAD_DIM
    return pl.ds(pl.multiple_of(lax.rem(index, SIDE) * wide, HEAD_DIM), wide)


def after(value, first):
    return lax.optimization_barrier((value, first))[0]


def column(index):
    return pl.ds(pl.multiple_of(index * HEAD_DIM, HEAD_DIM), HEAD_DIM)


def prep_kernel(z_ref, qkv_ref, gain_ref, cos_ref, sin_ref, main_ref, *shared):
    z = z_ref[0]
    cosine = cos_ref[...]
    sine = sin_ref[...]
    for part in range(3):
        if part < 2:
            total = jnp.zeros((TOK, HEAD_DIM), jnp.float32)
            for head in range(HEADS):
                x = qkv_ref[part, :, head * HEAD_DIM : (head + 1) * HEAD_DIM].astype(jnp.float32)
                total = total + x * x
            mean_sq = jnp.sum(total, axis=1, keepdims=True) / WIDTH
            inverse = lax.rsqrt(mean_sq + 1e-06)

        def head_of(cols):
            x = qkv_ref[part, :, cols]
            if part == 2:
                return x
            y = x.astype(jnp.float32) * inverse * gain_ref[part : part + 1, cols]
            turned = pltpu.roll(y, HEAD_DIM // 2, 1)
            return (y * cosine + turned * sine).astype(jnp.bfloat16)

        for step in range(SIDE):
            shared[step][part] = head_of(column(lax.rem(z + step, SIDE) * GROUP + GROUP - 1))
        for to_x in range(SIDE):
            for to_z in range(SIDE):
                at = (to_z * GROUP + to_x) * HEAD_DIM
                if part < 2:
                    main_ref[to_x * SIDE + to_z, part] = head_of(slice(at, at + HEAD_DIM))


def cut_values_kernel(v_ref, out_ref):
    for to_x in range(SIDE):
        for to_z in range(SIDE):
            at = (to_z * GROUP + to_x) * HEAD_DIM
            out_ref[to_x * SIDE + to_z] = v_ref[0, :, at : at + HEAD_DIM]


def cut_cotangent_kernel(z_ref, cot_ref, *outs):
    z = z_ref[0]
    for step in range(SIDE):
        outs[step][...] = cot_ref[:, group_columns(z + step)]


def attend(q, keys, values):
    nt = (((1,), (1,)), ((), ()))
    scores = [lax.dot_general(q, k, nt, preferred_element_type=jnp.float32) for k in keys]
    peak = functools.reduce(jnp.maximum, [jnp.max(s, axis=1, keepdims=True) for s in scores])
    expo = [jnp.exp2((s - peak) * EXP_SCALE) for s in scores]
    total = sum(jnp.sum(e, axis=1, keepdims=True) for e in expo)
    accum = sum(
        jnp.dot(e.astype(jnp.bfloat16), v, preferred_element_type=jnp.float32)
        for e, v in zip(expo, values, strict=True)
    )
    return (accum / total).astype(jnp.bfloat16)


def shared_kernel(q0, q1, q2, q3, s0, s1, s2, s3, out_ref):
    blocks = (s0, s1, s2, s3)
    for pair in ((q0, q1), (q2, q3)):
        at = 0 if pair[0] is q0 else TILE
        q = jnp.concatenate([p[0] for p in pair])
        out_ref[at : at + TILE] = attend(q, [b[0] for b in blocks], [b[1] for b in blocks])


def main_kernel(back, x_ref, r_ref, v_ref, *outs):
    x = x_ref[0]

    fours = [pl.ds(m * SIDE, SIDE) for m in range(SIDE)]
    keys = [r_ref[four, 1].reshape(ROWS, HEAD_DIM) for four in fours]
    values = [v_ref[four].reshape(ROWS, HEAD_DIM) for four in fours]
    for step, out_ref in zip(back, outs, strict=True):
        first = lax.rem(x + SIDE - step, SIDE) * SIDE
        for i in range(ROWS // TILE):
            half = SIDE // 2
            q = r_ref[pl.ds(first + i * half, half), 0].reshape(TILE, HEAD_DIM)
            out_ref[i * TILE : (i + 1) * TILE] = attend(q, keys, values)


def rows_of(z, source, step):
    first = lax.rem(z + SIDE - step, SIDE) if source < SIDE else step
    return pl.ds(pl.multiple_of(first * TOK, 32), TOK)


def join_kernel(place_ref, *refs):
    x, z = place_ref[0], place_ref[1]
    outs = refs[GROUP:]
    for source in range(GROUP):
        place = lax.rem(x + source, SIDE) if source < SIDE else SIDE
        for step in range(SIDE):
            outs[step][:, column(place)] = refs[source][rows_of(z, source, step)]


def channels_kernel(place_ref, time_ref, *refs):
    x, z = place_ref[0], place_ref[1]
    cots = refs[GROUP : GROUP + SIDE]
    out_ref, chan_ref = refs[GROUP + SIDE :]
    chan_ref[...] = jnp.zeros_like(chan_ref)
    for source in range(GROUP):
        place = lax.rem(x + source, SIDE) if source < SIDE else SIDE
        total = jnp.zeros((TOK, HEAD_DIM), jnp.float32)
        for step in range(SIDE):
            attn = refs[source][rows_of(z, source, step)].astype(jnp.float32)
            total = total + attn * cots[step][:, column(place)].astype(jnp.float32)
        chan_ref[pl.ds(place, 1)] = jnp.sum(total, axis=0, keepdims=True)
    chan_ref[GROUP : GROUP + 1] = time_ref[...]
    for i in range(out_ref.shape[0]):
        out_ref[i] = chan_ref[...]


def finish_kernel(z_ref, a0, a1, a2, a3, gate_ref, out_ref):
    z = z_ref[0]
    for step, a in enumerate((a0, a1, a2, a3)):
        cols = group_columns(z + step)
        out_ref[:, cols] = (a[...].astype(jnp.float32) * gate_ref[:, cols]).astype(jnp.bfloat16)


def grad_kernel(index_ref, freq_ref, before_ref, chan_ref, out_ref):
    is_cosine = index_ref[0] < FREQS // 2
    factors = []
    for d in range(SIDE):
        angle = chan_ref[d, GROUP : GROUP + 1] * freq_ref[...]
        factors.append(jnp.where(is_cosine, jnp.cos(angle), jnp.sin(angle)))
    for z in range(SIDE):
        chans = [sum(chan_ref[(x * SIDE + z) * SIDE + d] for x in range(SIDE)) for d in range(SIDE)]
        for head in range(GROUP):
            total = sum(f * c[head : head + 1] for f, c in zip(factors, chans, strict=True))
            at = (z * GROUP + head) * HEAD_DIM
            cols = slice(at, at + HEAD_DIM)
            out_ref[:, cols] = before_ref[...] + total


def shape(dims, dtype=jnp.bfloat16):
    return jax.ShapeDtypeStruct(dims, dtype)


def frequencies():
    count = FREQS // 2
    return (10000.0 ** (-np.arange(count) / count)).astype(np.float32)


def embed(step):
    angle = step.astype(jnp.float32) * frequencies()
    return jnp.concatenate([jnp.cos(angle), jnp.sin(angle)])


def local(qkv, qk_gain, mod_weight, positions, timesteps, cotangent):
    ctx = lax.axis_index("ctx").astype(jnp.int32)
    x = (ctx // SIDE)[None]
    z = (ctx % SIDE)[None]
    steps = (1, 2, 3)
    place = jnp.concatenate([x, z])
    count = SIDE * SIDE
    block = shape((3, TOK, HEAD_DIM))
    single = shape((ROWS, HEAD_DIM))
    flat = shape((TOK, GROUP * HEAD_DIM))

    step = timesteps[0, 0]
    when = jnp.full((1, HEAD_DIM), step.astype(jnp.float32))
    gains = lax.ppermute(qk_gain[0], "segment", [((i + 1) % SIDE, i) for i in range(SIDE)])
    parts = qkv[0, 0].transpose(1, 0, 2)
    cosine, sine = rope_tables(positions[0])
    values = call(
        cut_values_kernel,
        shape((count, TOK, HEAD_DIM)),
        0,
        1_600_000,
        parts,
        specs=[one_of(2, (TOK, WIDTH))],
    )
    values = lax.all_to_all(after(values, (gains, cosine, sine)), "ctx", 0, 0)
    main, *shared = call(
        prep_kernel,
        [shape((count, 2, TOK, HEAD_DIM))] + [block] * SIDE,
        10_000_000,
        5_000_000,
        z,
        parts,
        gains,
        cosine,
        sine,
    )
    cots = call(cut_cotangent_kernel, [flat] * SIDE, 0, 1_600_000, z, after(cotangent[0, 0], shared))
    cots_z = exchanged(along_z, cots)
    shared_z = exchanged(along_z, shared)
    main = lax.all_to_all(after(main, (values, shared_z, cots_z[3])), "ctx", 0, 0)
    pair = jnp.concatenate([b[1:] for b in shared_z], axis=1)
    pairs = [pair] + [along_x(pair, k) for k in steps]
    gate = jnp.dot(embed(step), mod_weight[0], precision=lax.Precision.HIGHEST)[None]
    rows = FREQS // (SIDE * SIDE * SIDE)
    index = (ctx * SIDE + lax.axis_index("dp").astype(jnp.int32)) * rows
    freq = lax.dynamic_slice_in_dim(np.tile(frequencies(), 2), index, rows)
    freq = jnp.broadcast_to(freq[:, None], (rows, HEAD_DIM))
    main, gate, freq = lax.optimization_barrier((main, gate, freq))
    back = [None] * SIDE
    back[2], back[1], back[3], back[0] = call(
        functools.partial(main_kernel, (2, 1, 3, 0)),
        [single] * SIDE,
        3_400_000_000,
        2_500_000,
        x,
        main,
        values,
    )
    shared_out = call(
        shared_kernel, single, 840_000_000, 1_600_000, *after(shared_z, (back[2], cots_z[1], cots_z[2])), *pairs, smem=0
    )
    for m in (2, 1, 3, 0):
        back[m] = onward(back[m], m)
    shared_out = onward(shared_out, 0)
    joined = call(
        join_kernel, [flat] * SIDE, 0, 1_600_000, place, *back, shared_out
    )
    at_home = [joined[0]] + [along_z(joined[k], SIDE - k) for k in steps]

    def gradient(_, state):
        attn, before = lax.optimization_barrier(([*back, shared_out], state[1]))
        chans = pl.pallas_call(
            channels_kernel,
            out_shape=shape((SIDE * count, 8, HEAD_DIM), jnp.float32),
            in_specs=[SMEM_SPEC] + [VMEM_SPEC] * (1 + GROUP + SIDE),
            out_specs=VMEM_SPEC,
            scratch_shapes=[pltpu.VMEM((8, HEAD_DIM), jnp.float32)],
            compiler_params=VMEM,
            cost_estimate=pl.CostEstimate(flops=0, bytes_accessed=0, transcendentals=0),
        )(place, when, *attn, *cots_z)
        chans = lax.all_to_all(chans, ("ctx", "dp"), 0, 0)
        grad = call(grad_kernel, zeros, 0, 200_000, index[None], freq, before, chans)
        return (grad, before)

    zeros = shape((rows, WIDTH), jnp.float32)
    turns = jnp.where(step < 1000, 1, 2)
    start = (jnp.zeros((rows, WIDTH), jnp.float32), jnp.zeros((rows, HEAD_DIM), jnp.float32))
    grad, _ = lax.fori_loop(0, turns, gradient, start)

    attn_out = call(
        finish_kernel, shape((TOK, WIDTH)), 500_000, 1_700_000, z, *after(at_home, grad), gate
    )
    return (attn_out[None, None], grad[None])


def solution(mesh):
    return jax.shard_map(
        local,
        mesh=mesh,
        in_specs=(
            P("segment", "dp", "ctx", None, None),
            P("segment", None, None),
            P("segment", None, None),
            P("dp", "ctx"),
            P("segment", "dp"),
            P("segment", "dp", "ctx", None),
        ),
        out_specs=(P("segment", "dp", "ctx", None), P("segment", ("ctx", "dp"), None)),
        check_vma=False,
    )
```

```python
import functools

import jax
import jax.numpy as jnp
import numpy as np
from jax import lax
from jax.experimental import pallas as pl
from jax.experimental.pallas import tpu as pltpu
from jax.sharding import PartitionSpec as P

HEADS = 20
HEAD_DIM = 128
FREQS = 256
GRID_ROWS = 45
GRID_COLS = 80
SIDE = 4
GROUP = HEADS // SIDE
TOK = 160
ROWS = SIDE * TOK
WIDTH = HEADS * HEAD_DIM
TILE = 320
EXP_SCALE = 1.4426950408889634 / HEAD_DIM**0.5
VMEM = pltpu.CompilerParams(vmem_limit_bytes=56 * 1024 * 1024)
SMEM_SPEC = pl.BlockSpec(memory_space=pltpu.SMEM)
VMEM_SPEC = pl.BlockSpec(memory_space=pltpu.VMEM)


def along_z(value, by):
    pairs = [(i, i // SIDE * SIDE + (i + by) % SIDE) for i in range(SIDE * SIDE)]
    return lax.ppermute(value, "ctx", pairs)


def along_x(value, by):
    pairs = [(i, (i + SIDE * by) % (SIDE * SIDE)) for i in range(SIDE * SIDE)]
    return lax.ppermute(value, "ctx", pairs)


def along_dp(value, by):
    return lax.ppermute(value, "dp", [(i, (i + by) % SIDE) for i in range(SIDE)])


def exchanged(along, blocks):
    got = list(blocks)
    for k in (2, 1, 3):
        got[k] = along(blocks[k], k)
    return got


def section_pairs(turn, by):
    count = SIDE * SIDE
    pairs = []
    for seg in range(SIDE):
        for i in range(count):
            target = (seg + turn) % SIDE * count + i // SIDE * SIDE + (i + by) % SIDE
            pairs.append((seg * count + i, target))
    return pairs


def home(value, by):
    return lax.ppermute(value, ("segment", "ctx"), section_pairs(1, by))


def away(value, by):
    return lax.ppermute(value, ("segment", "ctx"), section_pairs(SIDE - 1, by))


def rope_tables(pos):
    half = HEAD_DIM // 2
    side = HEAD_DIM // 6
    first = half - 2 * side
    frame = (pos // (GRID_ROWS * GRID_COLS)).astype(jnp.float32)
    row = (pos // GRID_COLS % GRID_ROWS).astype(jnp.float32)
    col = (pos % GRID_COLS).astype(jnp.float32)
    pair = np.arange(half)
    group = np.where(pair < first, 0, np.where(pair < first + side, 1, 2))
    offset = np.where(group == 0, 0, np.where(group == 1, first, first + side))
    pairs_in = np.where(group == 0, first, side)
    freq = (10000.0 ** (-(pair - offset) / pairs_in)).astype(np.float32)
    coord = jnp.where(
        group[None, :] == 0,
        frame[:, None],
        jnp.where(group[None, :] == 1, row[:, None], col[:, None]),
    )
    angle = coord * freq[None, :]
    cosine = jnp.concatenate([jnp.cos(angle), jnp.cos(angle)], axis=1)
    sine = jnp.concatenate([-jnp.sin(angle), jnp.sin(angle)], axis=1)
    return (cosine, sine)


def one_of(which, dims):
    return pl.BlockSpec((1, *dims), lambda i: (which, 0, 0))


def call(kernel, out_shape, flops, moved, *operands, smem=1, specs=None):
    grid = () if specs is None else (1,)
    specs = specs or [SMEM_SPEC] * smem + [VMEM_SPEC] * (len(operands) - smem)
    return pl.pallas_call(
        kernel,
        grid=grid,
        out_shape=out_shape,
        in_specs=specs,
        out_specs=jax.tree.map(lambda _: VMEM_SPEC, out_shape),
        compiler_params=VMEM,
        cost_estimate=pl.CostEstimate(flops=0, bytes_accessed=0, transcendentals=0),
    )(*operands)


def group_columns(index):
    wide = GROUP * HEAD_DIM
    return pl.ds(pl.multiple_of(lax.rem(index, SIDE) * wide, HEAD_DIM), wide)


def after(value, first):
    return lax.optimization_barrier((value, first))[0]


def column(index):
    return pl.ds(pl.multiple_of(index * HEAD_DIM, HEAD_DIM), HEAD_DIM)


def prep_kernel(z_ref, qkv_ref, gain_ref, cos_ref, sin_ref, main_ref, *shared):
    z = z_ref[0]
    cosine = cos_ref[...]
    sine = sin_ref[...]
    for part in range(3):
        if part < 2:
            total = jnp.zeros((TOK, HEAD_DIM), jnp.float32)
            for head in range(HEADS):
                x = qkv_ref[part, :, head * HEAD_DIM : (head + 1) * HEAD_DIM].astype(jnp.float32)
                total = total + x * x
            mean_sq = jnp.sum(total, axis=1, keepdims=True) / WIDTH
            inverse = lax.rsqrt(mean_sq + 1e-06)

        def head_of(cols):
            x = qkv_ref[part, :, cols]
            if part == 2:
                return x
            y = x.astype(jnp.float32) * inverse * gain_ref[part : part + 1, cols]
            turned = pltpu.roll(y, HEAD_DIM // 2, 1)
            return (y * cosine + turned * sine).astype(jnp.bfloat16)

        for step in range(SIDE):
            shared[step][part] = head_of(column(lax.rem(z + step, SIDE) * GROUP + GROUP - 1))
        for to_x in range(SIDE):
            for to_z in range(SIDE):
                at = (to_z * GROUP + to_x) * HEAD_DIM
                main_ref[to_x * SIDE + to_z, part] = head_of(slice(at, at + HEAD_DIM))


def cut_cotangent_kernel(z_ref, cot_ref, *outs):
    z = z_ref[0]
    for step in range(SIDE):
        outs[step][...] = cot_ref[:, group_columns(z + step)]


def attend(q, keys, values):
    nt = (((1,), (1,)), ((), ()))
    scores = [lax.dot_general(q, k, nt, preferred_element_type=jnp.float32) for k in keys]
    peak = functools.reduce(jnp.maximum, [jnp.max(s, axis=1, keepdims=True) for s in scores])
    expo = [jnp.exp2((s - peak) * EXP_SCALE) for s in scores]
    total = sum(jnp.sum(e, axis=1, keepdims=True) for e in expo)
    accum = sum(
        jnp.dot(e.astype(jnp.bfloat16), v, preferred_element_type=jnp.float32)
        for e, v in zip(expo, values, strict=True)
    )
    return (accum / total).astype(jnp.bfloat16)


def pack_kernel(s0, s1, s2, s3, out_ref):
    for j, s in enumerate((s0, s1, s2, s3)):
        for part in range(2):
            out_ref[part, j * TOK : (j + 1) * TOK] = s[part + 1]


def shared_kernel(q0, q1, q2, q3, s0, s1, s2, s3, out_ref):
    blocks = (s0, s1, s2, s3)
    for pair in ((q0, q1), (q2, q3)):
        at = 0 if pair[0] is q0 else TILE
        q = jnp.concatenate([p[0] for p in pair])
        out_ref[at : at + TILE] = attend(q, [b[0] for b in blocks], [b[1] for b in blocks])


def main_kernel(back, x_ref, r_ref, *outs):
    x = x_ref[0]

    def four(part, first):
        return r_ref[pl.ds(first * SIDE, SIDE), part].reshape(ROWS, HEAD_DIM)

    keys = [four(1, m) for m in range(SIDE)]
    values = [four(2, m) for m in range(SIDE)]
    for step, out_ref in zip(back, outs, strict=True):
        first = lax.rem(x + SIDE - step, SIDE) * SIDE
        for i in range(ROWS // TILE):
            half = SIDE // 2
            q = r_ref[pl.ds(first + i * half, half), 0].reshape(TILE, HEAD_DIM)
            out_ref[i * TILE : (i + 1) * TILE] = attend(q, keys, values)


def rows_of(z, source, step):
    first = lax.rem(z + SIDE - step, SIDE) if source < SIDE else step
    return pl.ds(pl.multiple_of(first * TOK, 32), TOK)


def join_kernel(place_ref, *refs):
    x, z = place_ref[0], place_ref[1]
    outs = refs[GROUP:]
    for source in range(GROUP):
        place = lax.rem(x + source, SIDE) if source < SIDE else SIDE
        for step in range(SIDE):
            outs[step][:, column(place)] = refs[source][rows_of(z, source, step)]


def channels_kernel(place_ref, time_ref, *refs):
    x, z = place_ref[0], place_ref[1]
    cots = refs[GROUP : GROUP + SIDE]
    out_ref, chan_ref = refs[GROUP + SIDE :]
    chan_ref[...] = jnp.zeros_like(chan_ref)
    for source in range(GROUP):
        place = lax.rem(x + source, SIDE) if source < SIDE else SIDE
        total = jnp.zeros((TOK, HEAD_DIM), jnp.float32)
        for step in range(SIDE):
            attn = refs[source][rows_of(z, source, step)].astype(jnp.float32)
            total = total + attn * cots[step][:, column(place)].astype(jnp.float32)
        chan_ref[pl.ds(place, 1)] = jnp.sum(total, axis=0, keepdims=True)
    chan_ref[GROUP : GROUP + 1] = time_ref[2:3, :HEAD_DIM]
    for i in range(out_ref.shape[0]):
        out_ref[i] = chan_ref[...]


def finish_kernel(z_ref, a0, a1, a2, a3, gate_ref, out_ref):
    z = z_ref[0]
    for step, a in enumerate((a0, a1, a2, a3)):
        cols = group_columns(z + step)
        out_ref[:, cols] = (a[...].astype(jnp.float32) * gate_ref[:, cols]).astype(jnp.bfloat16)


def grad_kernel(index_ref, freq_ref, before_ref, chan_ref, out_ref):
    is_cosine = index_ref[0] < FREQS // 2
    factors = []
    for d in range(SIDE):
        angle = chan_ref[d, GROUP : GROUP + 1] * freq_ref[...]
        factors.append(jnp.where(is_cosine, jnp.cos(angle), jnp.sin(angle)))
    for z in range(SIDE):
        chans = [sum(chan_ref[(x * SIDE + z) * SIDE + d] for x in range(SIDE)) for d in range(SIDE)]
        for head in range(GROUP):
            total = sum(f * c[head : head + 1] for f, c in zip(factors, chans, strict=True))
            at = (z * GROUP + head) * HEAD_DIM
            cols = slice(at, at + HEAD_DIM)
            out_ref[:, cols] = before_ref[...] + total


def shape(dims, dtype=jnp.bfloat16):
    return jax.ShapeDtypeStruct(dims, dtype)


def frequencies():
    count = FREQS // 2
    return (10000.0 ** (-np.arange(count) / count)).astype(np.float32)


def embed(step):
    angle = step.astype(jnp.float32) * frequencies()
    return jnp.concatenate([jnp.cos(angle), jnp.sin(angle)])


def local(qkv, qk_gain, mod_weight, positions, timesteps, cotangent):
    ctx = lax.axis_index("ctx").astype(jnp.int32)
    x = (ctx // SIDE)[None]
    z = (ctx % SIDE)[None]
    steps = (1, 2, 3)
    place = jnp.concatenate([x, z])
    count = SIDE * SIDE
    block = shape((3, TOK, HEAD_DIM))
    single = shape((ROWS, HEAD_DIM))
    flat = shape((TOK, GROUP * HEAD_DIM))

    step = timesteps[0, 0]
    when = jnp.full((1, WIDTH), step.astype(jnp.float32))
    gains = jnp.concatenate([qk_gain[0], when])
    gains = lax.ppermute(gains, "segment", [((i + 1) % SIDE, i) for i in range(SIDE)])
    parts = qkv[0, 0].transpose(1, 0, 2)
    cots = call(cut_cotangent_kernel, [flat] * SIDE, 0, 1_600_000, z, cotangent[0, 0])
    cots_z = [None] * SIDE
    cosine, sine = rope_tables(positions[0])
    main, *shared = call(
        prep_kernel,
        [shape((count, 3, TOK, HEAD_DIM))] + [block] * SIDE,
        10_000_000,
        5_000_000,
        z,
        parts,
        gains,
        cosine,
        sine,
    )
    shared_z = exchanged(along_z, shared)
    main = lax.all_to_all(main, "ctx", 0, 0)
    gate = jnp.dot(embed(step), mod_weight[0], precision=lax.Precision.HIGHEST)[None]
    rows = FREQS // (SIDE * SIDE * SIDE)
    index = (ctx * SIDE + lax.axis_index("dp").astype(jnp.int32)) * rows
    freq = lax.dynamic_slice_in_dim(np.tile(frequencies(), 2), index, rows)
    freq = jnp.broadcast_to(freq[:, None], (rows, HEAD_DIM))
    main, gate, freq = lax.optimization_barrier((main, gate, freq))
    back = [None] * SIDE
    back[2], back[1], back[3] = call(
        functools.partial(main_kernel, (2, 1, 3)), [single] * 3, 2_500_000_000, 2_500_000, x, main
    )
    (back[0],) = call(
        functools.partial(main_kernel, (0,)), [single], 840_000_000, 2_000_000, x, main
    )
    for k in (2, 1):
        cots_z[k] = away(after(cots[k], shared_z), k)
    pair = call(
        pack_kernel,
        shape((2, ROWS, HEAD_DIM)),
        0,
        1_300_000,
        *shared_z,
        smem=0,
    )
    pairs = [pair] + [along_x(pair, k) for k in steps]
    shared_out = call(
        shared_kernel, single, 840_000_000, 1_600_000, *shared_z, *pairs, smem=0
    )
    for k in (3, 0):
        cots_z[k] = away(after(cots[k], back[2]), k)
    back = [back[0]] + [along_x(back[m], SIDE - m) for m in steps]
    joined = call(
        join_kernel, [flat] * SIDE, 0, 1_600_000, place, *back, after(shared_out, cots_z[1:3])
    )
    at_home = [None] * SIDE
    for k in (2, 1, 3, 0):
        at_home[k] = home(joined[k], (SIDE - k) % SIDE)

    def gradient(_, state):
        attn, before = lax.optimization_barrier(([*back, shared_out], state[1]))
        chans = pl.pallas_call(
            channels_kernel,
            out_shape=shape((SIDE * count, 8, HEAD_DIM), jnp.float32),
            in_specs=[SMEM_SPEC] + [VMEM_SPEC] * (1 + GROUP + SIDE),
            out_specs=VMEM_SPEC,
            scratch_shapes=[pltpu.VMEM((8, HEAD_DIM), jnp.float32)],
            compiler_params=VMEM,
            cost_estimate=pl.CostEstimate(flops=0, bytes_accessed=0, transcendentals=0),
        )(place, gains, *attn, *cots_z)
        chans = lax.all_to_all(chans, ("ctx", "dp"), 0, 0)
        grad = call(grad_kernel, zeros, 0, 200_000, index[None], freq, before, chans)
        return (grad, before)

    zeros = shape((rows, WIDTH), jnp.float32)
    turns = jnp.where(step < 1000, 1, 2)
    start = (jnp.zeros((rows, WIDTH), jnp.float32), jnp.zeros((rows, HEAD_DIM), jnp.float32))
    grad, _ = lax.fori_loop(0, turns, gradient, start)
    grad = lax.ppermute(grad, "segment", [(i, (i + 1) % SIDE) for i in range(SIDE)])

    attn_out = call(
        finish_kernel, shape((TOK, WIDTH)), 500_000, 1_700_000, z, *at_home, gate
    )
    return (attn_out[None, None], grad[None])


def solution(mesh):
    return jax.shard_map(
        local,
        mesh=mesh,
        in_specs=(
            P("segment", "dp", "ctx", None, None),
            P("segment", None, None),
            P("segment", None, None),
            P("dp", "ctx"),
            P("segment", "dp"),
            P("segment", "dp", "ctx", None),
        ),
        out_specs=(P("segment", "dp", "ctx", None), P("segment", ("ctx", "dp"), None)),
        check_vma=False,
    )
```

```python
import functools

import jax
import jax.numpy as jnp
import numpy as np
from jax import lax
from jax.experimental import pallas as pl
from jax.experimental.pallas import tpu as pltpu
from jax.sharding import PartitionSpec as P

HEADS = 20
HEAD_DIM = 128
FREQS = 256
GRID_ROWS = 45
GRID_COLS = 80
SIDE = 4
GROUP = HEADS // SIDE
TOK = 160
ROWS = SIDE * TOK
WIDTH = HEADS * HEAD_DIM
TILE = 320
EXP_SCALE = 1.4426950408889634 / HEAD_DIM**0.5
VMEM = pltpu.CompilerParams(vmem_limit_bytes=56 * 1024 * 1024)
SMEM_SPEC = pl.BlockSpec(memory_space=pltpu.SMEM)
VMEM_SPEC = pl.BlockSpec(memory_space=pltpu.VMEM)


def along_z(value, by):
    pairs = [(i, i // SIDE * SIDE + (i + by) % SIDE) for i in range(SIDE * SIDE)]
    return lax.ppermute(value, "ctx", pairs)


def along_x(value, by):
    pairs = [(i, (i + SIDE * by) % (SIDE * SIDE)) for i in range(SIDE * SIDE)]
    return lax.ppermute(value, "ctx", pairs)


def along_dp(value, by):
    return lax.ppermute(value, "dp", [(i, (i + by) % SIDE) for i in range(SIDE)])


def exchanged(along, blocks):
    got = list(blocks)
    for k in (2, 1, 3):
        got[k] = along(blocks[k], k)
    return got


def section_pairs(turn, by):
    count = SIDE * SIDE
    pairs = []
    for seg in range(SIDE):
        for i in range(count):
            target = (seg + turn) % SIDE * count + i // SIDE * SIDE + (i + by) % SIDE
            pairs.append((seg * count + i, target))
    return pairs


def home(value, by):
    return lax.ppermute(value, ("segment", "ctx"), section_pairs(1, by))


def away(value, by):
    return lax.ppermute(value, ("segment", "ctx"), section_pairs(SIDE - 1, by))


def rope_tables(pos):
    half = HEAD_DIM // 2
    side = HEAD_DIM // 6
    first = half - 2 * side
    frame = (pos // (GRID_ROWS * GRID_COLS)).astype(jnp.float32)
    row = (pos // GRID_COLS % GRID_ROWS).astype(jnp.float32)
    col = (pos % GRID_COLS).astype(jnp.float32)
    pair = np.arange(half)
    group = np.where(pair < first, 0, np.where(pair < first + side, 1, 2))
    offset = np.where(group == 0, 0, np.where(group == 1, first, first + side))
    pairs_in = np.where(group == 0, first, side)
    freq = (10000.0 ** (-(pair - offset) / pairs_in)).astype(np.float32)
    coord = jnp.where(
        group[None, :] == 0,
        frame[:, None],
        jnp.where(group[None, :] == 1, row[:, None], col[:, None]),
    )
    angle = coord * freq[None, :]
    cosine = jnp.concatenate([jnp.cos(angle), jnp.cos(angle)], axis=1)
    sine = jnp.concatenate([-jnp.sin(angle), jnp.sin(angle)], axis=1)
    return (cosine, sine)


def one_of(which, dims):
    return pl.BlockSpec((1, *dims), lambda i: (which, 0, 0))


def call(kernel, out_shape, flops, moved, *operands, smem=1, specs=None):
    grid = () if specs is None else (1,)
    specs = specs or [SMEM_SPEC] * smem + [VMEM_SPEC] * (len(operands) - smem)
    return pl.pallas_call(
        kernel,
        grid=grid,
        out_shape=out_shape,
        in_specs=specs,
        out_specs=jax.tree.map(lambda _: VMEM_SPEC, out_shape),
        compiler_params=VMEM,
        cost_estimate=pl.CostEstimate(flops=0, bytes_accessed=0, transcendentals=0),
    )(*operands)


def group_columns(index):
    wide = GROUP * HEAD_DIM
    return pl.ds(pl.multiple_of(lax.rem(index, SIDE) * wide, HEAD_DIM), wide)


def after(value, first):
    return lax.optimization_barrier((value, first))[0]


def column(index):
    return pl.ds(pl.multiple_of(index * HEAD_DIM, HEAD_DIM), HEAD_DIM)


def prep_kernel(z_ref, qkv_ref, gain_ref, cos_ref, sin_ref, main_ref, *shared):
    z = z_ref[0]
    cosine = cos_ref[...]
    sine = sin_ref[...]
    for part in range(3):
        if part < 2:
            total = jnp.zeros((TOK, HEAD_DIM), jnp.float32)
            for head in range(HEADS):
                x = qkv_ref[part, :, head * HEAD_DIM : (head + 1) * HEAD_DIM].astype(jnp.float32)
                total = total + x * x
            mean_sq = jnp.sum(total, axis=1, keepdims=True) / WIDTH
            inverse = lax.rsqrt(mean_sq + 1e-06)

        def head_of(cols):
            x = qkv_ref[part, :, cols]
            if part == 2:
                return x
            y = x.astype(jnp.float32) * inverse * gain_ref[part : part + 1, cols]
            turned = pltpu.roll(y, HEAD_DIM // 2, 1)
            return (y * cosine + turned * sine).astype(jnp.bfloat16)

        for step in range(SIDE):
            shared[step][part] = head_of(column(lax.rem(z + step, SIDE) * GROUP + GROUP - 1))
        for to_x in range(SIDE):
            for to_z in range(SIDE):
                at = (to_z * GROUP + to_x) * HEAD_DIM
                main_ref[to_x * SIDE + to_z, part] = head_of(slice(at, at + HEAD_DIM))


def cut_cotangent_kernel(z_ref, cot_ref, *outs):
    z = z_ref[0]
    for step in range(SIDE):
        outs[step][...] = cot_ref[:, group_columns(z + step)]


def attend(q, keys, values):
    nt = (((1,), (1,)), ((), ()))
    scores = [lax.dot_general(q, k, nt, preferred_element_type=jnp.float32) for k in keys]
    peak = functools.reduce(jnp.maximum, [jnp.max(s, axis=1, keepdims=True) for s in scores])
    expo = [jnp.exp2((s - peak) * EXP_SCALE) for s in scores]
    total = sum(jnp.sum(e, axis=1, keepdims=True) for e in expo)
    accum = sum(
        jnp.dot(e.astype(jnp.bfloat16), v, preferred_element_type=jnp.float32)
        for e, v in zip(expo, values, strict=True)
    )
    return (accum / total).astype(jnp.bfloat16)


def pack_kernel(s0, s1, s2, s3, out_ref):
    for j, s in enumerate((s0, s1, s2, s3)):
        for part in range(2):
            out_ref[part, j * TOK : (j + 1) * TOK] = s[part + 1]


def shared_kernel(q0, q1, q2, q3, s0, s1, s2, s3, out_ref):
    blocks = (s0, s1, s2, s3)
    for pair in ((q0, q1), (q2, q3)):
        at = 0 if pair[0] is q0 else TILE
        q = jnp.concatenate([p[0] for p in pair])
        out_ref[at : at + TILE] = attend(q, [b[0] for b in blocks], [b[1] for b in blocks])


def main_kernel(back, x_ref, r_ref, *outs):
    x = x_ref[0]

    def four(part, first):
        return r_ref[pl.ds(first * SIDE, SIDE), part].reshape(ROWS, HEAD_DIM)

    keys = [four(1, m) for m in range(SIDE)]
    values = [four(2, m) for m in range(SIDE)]
    for step, out_ref in zip(back, outs, strict=True):
        first = lax.rem(x + SIDE - step, SIDE) * SIDE
        for i in range(ROWS // TILE):
            half = SIDE // 2
            q = r_ref[pl.ds(first + i * half, half), 0].reshape(TILE, HEAD_DIM)
            out_ref[i * TILE : (i + 1) * TILE] = attend(q, keys, values)


def rows_of(z, source, step):
    first = lax.rem(z + SIDE - step, SIDE) if source < SIDE else step
    return pl.ds(pl.multiple_of(first * TOK, 32), TOK)


def join_kernel(place_ref, *refs):
    x, z = place_ref[0], place_ref[1]
    outs = refs[GROUP:]
    for source in range(GROUP):
        place = lax.rem(x + source, SIDE) if source < SIDE else SIDE
        for step in range(SIDE):
            outs[step][:, column(place)] = refs[source][rows_of(z, source, step)]


def channels_kernel(place_ref, time_ref, *refs):
    x, z = place_ref[0], place_ref[1]
    cots = refs[GROUP : GROUP + SIDE]
    out_ref, chan_ref = refs[GROUP + SIDE :]
    chan_ref[...] = jnp.zeros_like(chan_ref)
    for source in range(GROUP):
        place = lax.rem(x + source, SIDE) if source < SIDE else SIDE
        total = jnp.zeros((TOK, HEAD_DIM), jnp.float32)
        for step in range(SIDE):
            attn = refs[source][rows_of(z, source, step)].astype(jnp.float32)
            total = total + attn * cots[step][:, column(place)].astype(jnp.float32)
        chan_ref[pl.ds(place, 1)] = jnp.sum(total, axis=0, keepdims=True)
    chan_ref[GROUP : GROUP + 1] = time_ref[2:3, :HEAD_DIM]
    for i in range(out_ref.shape[0]):
        out_ref[i] = chan_ref[...]


def finish_kernel(z_ref, a0, a1, a2, a3, gate_ref, out_ref):
    z = z_ref[0]
    for step, a in enumerate((a0, a1, a2, a3)):
        cols = group_columns(z + step)
        out_ref[:, cols] = (a[...].astype(jnp.float32) * gate_ref[:, cols]).astype(jnp.bfloat16)


def grad_kernel(index_ref, freq_ref, before_ref, chan_ref, out_ref):
    is_cosine = index_ref[0] < FREQS // 2
    factors = []
    for d in range(SIDE):
        angle = chan_ref[d, GROUP : GROUP + 1] * freq_ref[...]
        factors.append(jnp.where(is_cosine, jnp.cos(angle), jnp.sin(angle)))
    for z in range(SIDE):
        chans = [sum(chan_ref[(x * SIDE + z) * SIDE + d] for x in range(SIDE)) for d in range(SIDE)]
        for head in range(GROUP):
            total = sum(f * c[head : head + 1] for f, c in zip(factors, chans, strict=True))
            at = (z * GROUP + head) * HEAD_DIM
            cols = slice(at, at + HEAD_DIM)
            out_ref[:, cols] = before_ref[...] + total


def shape(dims, dtype=jnp.bfloat16):
    return jax.ShapeDtypeStruct(dims, dtype)


def frequencies():
    count = FREQS // 2
    return (10000.0 ** (-np.arange(count) / count)).astype(np.float32)


def embed(step):
    angle = step.astype(jnp.float32) * frequencies()
    return jnp.concatenate([jnp.cos(angle), jnp.sin(angle)])


def local(qkv, qk_gain, mod_weight, positions, timesteps, cotangent):
    ctx = lax.axis_index("ctx").astype(jnp.int32)
    x = (ctx // SIDE)[None]
    z = (ctx % SIDE)[None]
    steps = (1, 2, 3)
    place = jnp.concatenate([x, z])
    count = SIDE * SIDE
    block = shape((3, TOK, HEAD_DIM))
    single = shape((ROWS, HEAD_DIM))
    flat = shape((TOK, GROUP * HEAD_DIM))

    step = timesteps[0, 0]
    when = jnp.full((1, WIDTH), step.astype(jnp.float32))
    gains = jnp.concatenate([qk_gain[0], when])
    gains = lax.ppermute(gains, "segment", [((i + 1) % SIDE, i) for i in range(SIDE)])
    parts = qkv[0, 0].transpose(1, 0, 2)
    cots = call(cut_cotangent_kernel, [flat] * SIDE, 0, 1_600_000, z, cotangent[0, 0])
    cots_z = [None] * SIDE
    for k in (2, 0):
        cots_z[k] = away(cots[k], k)
    cosine, sine = rope_tables(positions[0])
    main, *shared = call(
        prep_kernel,
        [shape((count, 3, TOK, HEAD_DIM))] + [block] * SIDE,
        10_000_000,
        5_000_000,
        z,
        parts,
        gains,
        cosine,
        sine,
    )
    shared_z = exchanged(along_z, shared)
    prepared = shared
    main = lax.all_to_all(after(main, (cots_z[0], cots_z[2])), "ctx", 0, 0)
    gate = jnp.dot(embed(step), mod_weight[0], precision=lax.Precision.HIGHEST)[None]
    rows = FREQS // (SIDE * SIDE * SIDE)
    index = (ctx * SIDE + lax.axis_index("dp").astype(jnp.int32)) * rows
    freq = lax.dynamic_slice_in_dim(np.tile(frequencies(), 2), index, rows)
    freq = jnp.broadcast_to(freq[:, None], (rows, HEAD_DIM))
    main, gate, freq = lax.optimization_barrier((main, gate, freq))
    back = [None] * SIDE
    back[2], back[1], back[3] = call(
        functools.partial(main_kernel, (2, 1, 3)), [single] * 3, 2_500_000_000, 2_500_000, x, main
    )
    (back[0],) = call(
        functools.partial(main_kernel, (0,)), [single], 840_000_000, 2_000_000, x, main
    )
    for k in (1, 3):
        cots_z[k] = away(after(cots[k], prepared), k)
    pair = call(
        pack_kernel,
        shape((2, ROWS, HEAD_DIM)),
        0,
        1_300_000,
        *after(shared_z, (back[2], cots_z[1], cots_z[3])),
        smem=0,
    )
    pairs = [pair] + [along_x(pair, k) for k in steps]
    shared_out = call(
        shared_kernel, single, 840_000_000, 1_600_000, *shared_z, *pairs, smem=0
    )
    back = [back[0]] + [along_x(back[m], SIDE - m) for m in steps]
    joined = call(
        join_kernel, [flat] * SIDE, 0, 1_600_000, place, *back, shared_out
    )
    at_home = [None] * SIDE
    for k in (2, 1, 3, 0):
        at_home[k] = home(joined[k], (SIDE - k) % SIDE)

    def gradient(_, state):
        attn, before = lax.optimization_barrier(([*back, shared_out], state[1]))
        chans = pl.pallas_call(
            channels_kernel,
            out_shape=shape((SIDE * count, 8, HEAD_DIM), jnp.float32),
            in_specs=[SMEM_SPEC] + [VMEM_SPEC] * (1 + GROUP + SIDE),
            out_specs=VMEM_SPEC,
            scratch_shapes=[pltpu.VMEM((8, HEAD_DIM), jnp.float32)],
            compiler_params=VMEM,
            cost_estimate=pl.CostEstimate(flops=0, bytes_accessed=0, transcendentals=0),
        )(place, gains, *attn, *cots_z)
        chans = lax.all_to_all(chans, ("ctx", "dp"), 0, 0)
        grad = call(grad_kernel, zeros, 0, 200_000, index[None], freq, before, chans)
        return (grad, before)

    zeros = shape((rows, WIDTH), jnp.float32)
    turns = jnp.where(step < 1000, 1, 2)
    start = (jnp.zeros((rows, WIDTH), jnp.float32), jnp.zeros((rows, HEAD_DIM), jnp.float32))
    grad, _ = lax.fori_loop(0, turns, gradient, start)
    grad = lax.ppermute(grad, "segment", [(i, (i + 1) % SIDE) for i in range(SIDE)])

    attn_out = call(
        finish_kernel, shape((TOK, WIDTH)), 500_000, 1_700_000, z, *at_home, gate
    )
    return (attn_out[None, None], grad[None])


def solution(mesh):
    return jax.shard_map(
        local,
        mesh=mesh,
        in_specs=(
            P("segment", "dp", "ctx", None, None),
            P("segment", None, None),
            P("segment", None, None),
            P("dp", "ctx"),
            P("segment", "dp"),
            P("segment", "dp", "ctx", None),
        ),
        out_specs=(P("segment", "dp", "ctx", None), P("segment", ("ctx", "dp"), None)),
        check_vma=False,
    )
```

```python
import functools

import jax
import jax.numpy as jnp
import numpy as np
from jax import lax
from jax.experimental import pallas as pl
from jax.experimental.pallas import tpu as pltpu
from jax.sharding import PartitionSpec as P

HEADS = 20
HEAD_DIM = 128
FREQS = 256
GRID_ROWS = 45
GRID_COLS = 80
SIDE = 4
GROUP = HEADS // SIDE
TOK = 160
ROWS = SIDE * TOK
WIDTH = HEADS * HEAD_DIM
TILE = 320
EXP_SCALE = 1.4426950408889634 / HEAD_DIM**0.5
VMEM = pltpu.CompilerParams(vmem_limit_bytes=56 * 1024 * 1024)
SMEM_SPEC = pl.BlockSpec(memory_space=pltpu.SMEM)
VMEM_SPEC = pl.BlockSpec(memory_space=pltpu.VMEM)


def along_z(value, by):
    pairs = [(i, i // SIDE * SIDE + (i + by) % SIDE) for i in range(SIDE * SIDE)]
    return lax.ppermute(value, "ctx", pairs)


def along_x(value, by):
    pairs = [(i, (i + SIDE * by) % (SIDE * SIDE)) for i in range(SIDE * SIDE)]
    return lax.ppermute(value, "ctx", pairs)


def along_dp(value, by):
    return lax.ppermute(value, "dp", [(i, (i + by) % SIDE) for i in range(SIDE)])


def exchanged(along, blocks):
    got = list(blocks)
    for k in (2, 1, 3):
        got[k] = along(blocks[k], k)
    return got


def section_pairs(turn, by):
    count = SIDE * SIDE
    pairs = []
    for seg in range(SIDE):
        for i in range(count):
            target = (seg + turn) % SIDE * count + i // SIDE * SIDE + (i + by) % SIDE
            pairs.append((seg * count + i, target))
    return pairs


def home(value, by):
    return lax.ppermute(value, ("segment", "ctx"), section_pairs(1, by))


def away(value, by):
    return lax.ppermute(value, ("segment", "ctx"), section_pairs(SIDE - 1, by))


def rope_tables(pos):
    half = HEAD_DIM // 2
    side = HEAD_DIM // 6
    first = half - 2 * side
    frame = (pos // (GRID_ROWS * GRID_COLS)).astype(jnp.float32)
    row = (pos // GRID_COLS % GRID_ROWS).astype(jnp.float32)
    col = (pos % GRID_COLS).astype(jnp.float32)
    pair = np.arange(half)
    group = np.where(pair < first, 0, np.where(pair < first + side, 1, 2))
    offset = np.where(group == 0, 0, np.where(group == 1, first, first + side))
    pairs_in = np.where(group == 0, first, side)
    freq = (10000.0 ** (-(pair - offset) / pairs_in)).astype(np.float32)
    coord = jnp.where(
        group[None, :] == 0,
        frame[:, None],
        jnp.where(group[None, :] == 1, row[:, None], col[:, None]),
    )
    angle = coord * freq[None, :]
    cosine = jnp.concatenate([jnp.cos(angle), jnp.cos(angle)], axis=1)
    sine = jnp.concatenate([-jnp.sin(angle), jnp.sin(angle)], axis=1)
    return (cosine, sine)


def one_of(which, dims):
    return pl.BlockSpec((1, *dims), lambda i: (which, 0, 0))


def call(kernel, out_shape, flops, moved, *operands, smem=1, specs=None):
    grid = () if specs is None else (1,)
    specs = specs or [SMEM_SPEC] * smem + [VMEM_SPEC] * (len(operands) - smem)
    return pl.pallas_call(
        kernel,
        grid=grid,
        out_shape=out_shape,
        in_specs=specs,
        out_specs=jax.tree.map(lambda _: VMEM_SPEC, out_shape),
        compiler_params=VMEM,
        cost_estimate=pl.CostEstimate(flops=0, bytes_accessed=0, transcendentals=0),
    )(*operands)


def group_columns(index):
    wide = GROUP * HEAD_DIM
    return pl.ds(pl.multiple_of(lax.rem(index, SIDE) * wide, HEAD_DIM), wide)


def after(value, first):
    return lax.optimization_barrier((value, first))[0]


def column(index):
    return pl.ds(pl.multiple_of(index * HEAD_DIM, HEAD_DIM), HEAD_DIM)


def prep_kernel(z_ref, qkv_ref, gain_ref, cos_ref, sin_ref, main_ref, *shared):
    z = z_ref[0]
    cosine = cos_ref[...]
    sine = sin_ref[...]
    for part in range(3):
        if part < 2:
            total = jnp.zeros((TOK, HEAD_DIM), jnp.float32)
            for head in range(HEADS):
                x = qkv_ref[part, :, head * HEAD_DIM : (head + 1) * HEAD_DIM].astype(jnp.float32)
                total = total + x * x
            mean_sq = jnp.sum(total, axis=1, keepdims=True) / WIDTH
            inverse = lax.rsqrt(mean_sq + 1e-06)

        def head_of(cols):
            x = qkv_ref[part, :, cols]
            if part == 2:
                return x
            y = x.astype(jnp.float32) * inverse * gain_ref[part : part + 1, cols]
            turned = pltpu.roll(y, HEAD_DIM // 2, 1)
            return (y * cosine + turned * sine).astype(jnp.bfloat16)

        for step in range(SIDE):
            shared[step][part] = head_of(column(lax.rem(z + step, SIDE) * GROUP + GROUP - 1))
        for to_x in range(SIDE):
            for to_z in range(SIDE):
                at = (to_z * GROUP + to_x) * HEAD_DIM
                main_ref[to_x * SIDE + to_z, part] = head_of(slice(at, at + HEAD_DIM))


def cut_cotangent_kernel(z_ref, cot_ref, *outs):
    z = z_ref[0]
    for step in range(SIDE):
        outs[step][...] = cot_ref[:, group_columns(z + step)]


def attend(q, keys, values):
    nt = (((1,), (1,)), ((), ()))
    scores = [lax.dot_general(q, k, nt, preferred_element_type=jnp.float32) for k in keys]
    peak = functools.reduce(jnp.maximum, [jnp.max(s, axis=1, keepdims=True) for s in scores])
    expo = [jnp.exp2((s - peak) * EXP_SCALE) for s in scores]
    total = sum(jnp.sum(e, axis=1, keepdims=True) for e in expo)
    accum = sum(
        jnp.dot(e.astype(jnp.bfloat16), v, preferred_element_type=jnp.float32)
        for e, v in zip(expo, values, strict=True)
    )
    return (accum / total).astype(jnp.bfloat16)


def shared_kernel(q0, q1, q2, q3, s0, s1, s2, s3, out_ref):
    blocks = (s0, s1, s2, s3)
    for pair in ((q0, q1), (q2, q3)):
        at = 0 if pair[0] is q0 else TILE
        q = jnp.concatenate([p[0] for p in pair])
        out_ref[at : at + TILE] = attend(q, [b[0] for b in blocks], [b[1] for b in blocks])


def main_kernel(back, x_ref, r_ref, *outs):
    x = x_ref[0]

    def four(part, first):
        return r_ref[pl.ds(first * SIDE, SIDE), part].reshape(ROWS, HEAD_DIM)

    keys = [four(1, m) for m in range(SIDE)]
    values = [four(2, m) for m in range(SIDE)]
    for step, out_ref in zip(back, outs, strict=True):
        first = lax.rem(x + SIDE - step, SIDE) * SIDE
        for i in range(ROWS // TILE):
            half = SIDE // 2
            q = r_ref[pl.ds(first + i * half, half), 0].reshape(TILE, HEAD_DIM)
            out_ref[i * TILE : (i + 1) * TILE] = attend(q, keys, values)


def rows_of(z, source, step):
    first = lax.rem(z + SIDE - step, SIDE) if source < SIDE else step
    return pl.ds(pl.multiple_of(first * TOK, 32), TOK)


def join_kernel(place_ref, *refs):
    x, z = place_ref[0], place_ref[1]
    outs = refs[GROUP:]
    for source in range(GROUP):
        place = lax.rem(x + source, SIDE) if source < SIDE else SIDE
        for step in range(SIDE):
            outs[step][:, column(place)] = refs[source][rows_of(z, source, step)]


def channels_kernel(place_ref, time_ref, *refs):
    x, z = place_ref[0], place_ref[1]
    cots = refs[GROUP : GROUP + SIDE]
    out_ref, chan_ref = refs[GROUP + SIDE :]
    chan_ref[...] = jnp.zeros_like(chan_ref)
    for source in range(GROUP):
        place = lax.rem(x + source, SIDE) if source < SIDE else SIDE
        total = jnp.zeros((TOK, HEAD_DIM), jnp.float32)
        for step in range(SIDE):
            attn = refs[source][rows_of(z, source, step)].astype(jnp.float32)
            total = total + attn * cots[step][:, column(place)].astype(jnp.float32)
        chan_ref[pl.ds(place, 1)] = jnp.sum(total, axis=0, keepdims=True)
    chan_ref[GROUP : GROUP + 1] = time_ref[2:3, :HEAD_DIM]
    for i in range(out_ref.shape[0]):
        out_ref[i] = chan_ref[...]


def finish_kernel(z_ref, a0, a1, a2, a3, gate_ref, out_ref):
    z = z_ref[0]
    for step, a in enumerate((a0, a1, a2, a3)):
        cols = group_columns(z + step)
        out_ref[:, cols] = (a[...].astype(jnp.float32) * gate_ref[:, cols]).astype(jnp.bfloat16)


def grad_kernel(index_ref, freq_ref, before_ref, chan_ref, out_ref):
    is_cosine = index_ref[0] < FREQS // 2
    factors = []
    for d in range(SIDE):
        angle = chan_ref[d, GROUP : GROUP + 1] * freq_ref[...]
        factors.append(jnp.where(is_cosine, jnp.cos(angle), jnp.sin(angle)))
    for z in range(SIDE):
        chans = [sum(chan_ref[(x * SIDE + z) * SIDE + d] for x in range(SIDE)) for d in range(SIDE)]
        for head in range(GROUP):
            total = sum(f * c[head : head + 1] for f, c in zip(factors, chans, strict=True))
            at = (z * GROUP + head) * HEAD_DIM
            cols = slice(at, at + HEAD_DIM)
            out_ref[:, cols] = before_ref[...] + total


def shape(dims, dtype=jnp.bfloat16):
    return jax.ShapeDtypeStruct(dims, dtype)


def frequencies():
    count = FREQS // 2
    return (10000.0 ** (-np.arange(count) / count)).astype(np.float32)


def embed(step):
    angle = step.astype(jnp.float32) * frequencies()
    return jnp.concatenate([jnp.cos(angle), jnp.sin(angle)])


def local(qkv, qk_gain, mod_weight, positions, timesteps, cotangent):
    ctx = lax.axis_index("ctx").astype(jnp.int32)
    x = (ctx // SIDE)[None]
    z = (ctx % SIDE)[None]
    steps = (1, 2, 3)
    place = jnp.concatenate([x, z])
    count = SIDE * SIDE
    block = shape((3, TOK, HEAD_DIM))
    single = shape((ROWS, HEAD_DIM))
    flat = shape((TOK, GROUP * HEAD_DIM))

    step = timesteps[0, 0]
    when = jnp.full((1, WIDTH), step.astype(jnp.float32))
    gains = jnp.concatenate([qk_gain[0], when])
    gains = lax.ppermute(gains, "segment", [((i + 1) % SIDE, i) for i in range(SIDE)])
    parts = qkv[0, 0].transpose(1, 0, 2)
    cots = call(cut_cotangent_kernel, [flat] * SIDE, 0, 1_600_000, z, cotangent[0, 0])
    cots_z = [None] * SIDE
    for k in (2, 1):
        cots_z[k] = away(cots[k], k)
    cosine, sine = rope_tables(positions[0])
    main, *shared = call(
        prep_kernel,
        [shape((count, 3, TOK, HEAD_DIM))] + [block] * SIDE,
        10_000_000,
        5_000_000,
        z,
        parts,
        gains,
        cosine,
        sine,
    )
    shared_z = exchanged(along_z, shared)
    main = lax.all_to_all(after(main, shared_z), "ctx", 0, 0)
    pair = jnp.concatenate([b[1:] for b in shared_z], axis=1)
    pairs = [pair] + [along_x(pair, k) for k in steps]
    gate = jnp.dot(embed(step), mod_weight[0], precision=lax.Precision.HIGHEST)[None]
    rows = FREQS // (SIDE * SIDE * SIDE)
    index = (ctx * SIDE + lax.axis_index("dp").astype(jnp.int32)) * rows
    freq = lax.dynamic_slice_in_dim(np.tile(frequencies(), 2), index, rows)
    freq = jnp.broadcast_to(freq[:, None], (rows, HEAD_DIM))
    shared_out = call(
        shared_kernel, single, 840_000_000, 1_600_000, *shared_z, *pairs, smem=0
    )
    main, gate, freq = lax.optimization_barrier((main, gate, freq))
    back = [None] * SIDE
    back[2], back[1], back[3] = call(
        functools.partial(main_kernel, (2, 1, 3)), [single] * 3, 2_500_000_000, 2_500_000, x, main
    )
    (back[0],) = call(
        functools.partial(main_kernel, (0,)), [single], 840_000_000, 2_000_000, x, main
    )
    for k in (3, 0):
        cots_z[k] = away(after(cots[k], back[2]), k)
    back = [back[0]] + [along_x(back[m], SIDE - m) for m in steps]
    joined = call(
        join_kernel, [flat] * SIDE, 0, 1_600_000, place, *back, after(shared_out, cots_z[1:3])
    )
    at_home = [None] * SIDE
    for k in (2, 1, 3, 0):
        at_home[k] = home(joined[k], (SIDE - k) % SIDE)

    sums = pl.pallas_call(
        channels_kernel,
        out_shape=shape((SIDE * count, 8, HEAD_DIM), jnp.float32),
        in_specs=[SMEM_SPEC] + [VMEM_SPEC] * (1 + GROUP + SIDE),
        out_specs=VMEM_SPEC,
        scratch_shapes=[pltpu.VMEM((8, HEAD_DIM), jnp.float32)],
        compiler_params=VMEM,
        cost_estimate=pl.CostEstimate(flops=0, bytes_accessed=0, transcendentals=0),
    )(place, gains, *back, shared_out, *cots_z)
    sums = home(sums, 0)

    def gradient(_, state):
        mine, before = lax.optimization_barrier((sums, state[1]))
        chans = lax.all_to_all(mine, ("ctx", "dp"), 0, 0)
        grad = call(grad_kernel, zeros, 0, 200_000, index[None], freq, before, chans)
        return (grad, before)

    zeros = shape((rows, WIDTH), jnp.float32)
    turns = jnp.where(step < 1000, 1, 2)
    start = (jnp.zeros((rows, WIDTH), jnp.float32), jnp.zeros((rows, HEAD_DIM), jnp.float32))
    grad, _ = lax.fori_loop(0, turns, gradient, start)

    attn_out = call(
        finish_kernel, shape((TOK, WIDTH)), 500_000, 1_700_000, z, *at_home, after(gate, grad)
    )
    return (attn_out[None, None], grad[None])


def solution(mesh):
    return jax.shard_map(
        local,
        mesh=mesh,
        in_specs=(
            P("segment", "dp", "ctx", None, None),
            P("segment", None, None),
            P("segment", None, None),
            P("dp", "ctx"),
            P("segment", "dp"),
            P("segment", "dp", "ctx", None),
        ),
        out_specs=(P("segment", "dp", "ctx", None), P("segment", ("ctx", "dp"), None)),
        check_vma=False,
    )
```

```python
import functools

import jax
import jax.numpy as jnp
import numpy as np
from jax import lax
from jax.experimental import pallas as pl
from jax.experimental.pallas import tpu as pltpu
from jax.sharding import PartitionSpec as P

HEADS = 20
HEAD_DIM = 128
FREQS = 256
GRID_ROWS = 45
GRID_COLS = 80
SIDE = 4
GROUP = HEADS // SIDE
TOK = 160
ROWS = SIDE * TOK
WIDTH = HEADS * HEAD_DIM
TILE = 320
EXP_SCALE = 1.4426950408889634 / HEAD_DIM**0.5
VMEM = pltpu.CompilerParams(vmem_limit_bytes=56 * 1024 * 1024)
SMEM_SPEC = pl.BlockSpec(memory_space=pltpu.SMEM)
VMEM_SPEC = pl.BlockSpec(memory_space=pltpu.VMEM)


def along_z(value, by):
    pairs = [(i, i // SIDE * SIDE + (i + by) % SIDE) for i in range(SIDE * SIDE)]
    return lax.ppermute(value, "ctx", pairs)


def along_x(value, by):
    pairs = [(i, (i + SIDE * by) % (SIDE * SIDE)) for i in range(SIDE * SIDE)]
    return lax.ppermute(value, "ctx", pairs)


def along_dp(value, by):
    return lax.ppermute(value, "dp", [(i, (i + by) % SIDE) for i in range(SIDE)])


def exchanged(along, blocks):
    got = list(blocks)
    for k in (2, 1, 3):
        got[k] = along(blocks[k], k)
    return got


def section_pairs(turn, by):
    count = SIDE * SIDE
    pairs = []
    for seg in range(SIDE):
        for i in range(count):
            target = (seg + turn) % SIDE * count + i // SIDE * SIDE + (i + by) % SIDE
            pairs.append((seg * count + i, target))
    return pairs


def home(value, by):
    return lax.ppermute(value, ("segment", "ctx"), section_pairs(1, by))


def away(value, by):
    return lax.ppermute(value, ("segment", "ctx"), section_pairs(SIDE - 1, by))


def rope_tables(pos):
    half = HEAD_DIM // 2
    side = HEAD_DIM // 6
    first = half - 2 * side
    frame = (pos // (GRID_ROWS * GRID_COLS)).astype(jnp.float32)
    row = (pos // GRID_COLS % GRID_ROWS).astype(jnp.float32)
    col = (pos % GRID_COLS).astype(jnp.float32)
    pair = np.arange(half)
    group = np.where(pair < first, 0, np.where(pair < first + side, 1, 2))
    offset = np.where(group == 0, 0, np.where(group == 1, first, first + side))
    pairs_in = np.where(group == 0, first, side)
    freq = (10000.0 ** (-(pair - offset) / pairs_in)).astype(np.float32)
    coord = jnp.where(
        group[None, :] == 0,
        frame[:, None],
        jnp.where(group[None, :] == 1, row[:, None], col[:, None]),
    )
    angle = coord * freq[None, :]
    cosine = jnp.concatenate([jnp.cos(angle), jnp.cos(angle)], axis=1)
    sine = jnp.concatenate([-jnp.sin(angle), jnp.sin(angle)], axis=1)
    return (cosine, sine)


def one_of(which, dims):
    return pl.BlockSpec((1, *dims), lambda i: (which, 0, 0))


def call(kernel, out_shape, flops, moved, *operands, smem=1, specs=None):
    grid = () if specs is None else (1,)
    specs = specs or [SMEM_SPEC] * smem + [VMEM_SPEC] * (len(operands) - smem)
    return pl.pallas_call(
        kernel,
        grid=grid,
        out_shape=out_shape,
        in_specs=specs,
        out_specs=jax.tree.map(lambda _: VMEM_SPEC, out_shape),
        compiler_params=VMEM,
        cost_estimate=pl.CostEstimate(flops=0, bytes_accessed=0, transcendentals=0),
    )(*operands)


def group_columns(index):
    wide = GROUP * HEAD_DIM
    return pl.ds(pl.multiple_of(lax.rem(index, SIDE) * wide, HEAD_DIM), wide)


def after(value, first):
    return lax.optimization_barrier((value, first))[0]


def column(index):
    return pl.ds(pl.multiple_of(index * HEAD_DIM, HEAD_DIM), HEAD_DIM)


def prep_kernel(z_ref, qkv_ref, gain_ref, cos_ref, sin_ref, main_ref, *shared):
    z = z_ref[0]
    cosine = cos_ref[...]
    sine = sin_ref[...]
    for part in range(3):
        if part < 2:
            total = jnp.zeros((TOK, HEAD_DIM), jnp.float32)
            for head in range(HEADS):
                x = qkv_ref[part, :, head * HEAD_DIM : (head + 1) * HEAD_DIM].astype(jnp.float32)
                total = total + x * x
            mean_sq = jnp.sum(total, axis=1, keepdims=True) / WIDTH
            inverse = lax.rsqrt(mean_sq + 1e-06)

        def head_of(cols):
            x = qkv_ref[part, :, cols]
            if part == 2:
                return x
            y = x.astype(jnp.float32) * inverse * gain_ref[part : part + 1, cols]
            turned = pltpu.roll(y, HEAD_DIM // 2, 1)
            return (y * cosine + turned * sine).astype(jnp.bfloat16)

        for step in range(SIDE):
            shared[step][part] = head_of(column(lax.rem(z + step, SIDE) * GROUP + GROUP - 1))
        for to_x in range(SIDE):
            for to_z in range(SIDE):
                at = (to_z * GROUP + to_x) * HEAD_DIM
                main_ref[to_x * SIDE + to_z, part] = head_of(slice(at, at + HEAD_DIM))


def cut_cotangent_kernel(z_ref, cot_ref, *outs):
    z = z_ref[0]
    for step in range(SIDE):
        outs[step][...] = cot_ref[:, group_columns(z + step)]


def attend(q, keys, values):
    nt = (((1,), (1,)), ((), ()))
    scores = [lax.dot_general(q, k, nt, preferred_element_type=jnp.float32) for k in keys]
    peak = functools.reduce(jnp.maximum, [jnp.max(s, axis=1, keepdims=True) for s in scores])
    expo = [jnp.exp2((s - peak) * EXP_SCALE) for s in scores]
    total = sum(jnp.sum(e, axis=1, keepdims=True) for e in expo)
    accum = sum(
        jnp.dot(e.astype(jnp.bfloat16), v, preferred_element_type=jnp.float32)
        for e, v in zip(expo, values, strict=True)
    )
    return (accum / total).astype(jnp.bfloat16)


def shared_kernel(q0, q1, q2, q3, s0, s1, s2, s3, out_ref):
    blocks = (s0, s1, s2, s3)
    for pair in ((q0, q1), (q2, q3)):
        at = 0 if pair[0] is q0 else TILE
        q = jnp.concatenate([p[0] for p in pair])
        out_ref[at : at + TILE] = attend(q, [b[0] for b in blocks], [b[1] for b in blocks])


def main_kernel(back, x_ref, r_ref, *outs):
    x = x_ref[0]

    def four(part, first):
        return r_ref[pl.ds(first * SIDE, SIDE), part].reshape(ROWS, HEAD_DIM)

    keys = [four(1, m) for m in range(SIDE)]
    values = [four(2, m) for m in range(SIDE)]
    for step, out_ref in zip(back, outs, strict=True):
        first = lax.rem(x + SIDE - step, SIDE) * SIDE
        for i in range(ROWS // TILE):
            half = SIDE // 2
            q = r_ref[pl.ds(first + i * half, half), 0].reshape(TILE, HEAD_DIM)
            out_ref[i * TILE : (i + 1) * TILE] = attend(q, keys, values)


def rows_of(z, source, step):
    first = lax.rem(z + SIDE - step, SIDE) if source < SIDE else step
    return pl.ds(pl.multiple_of(first * TOK, 32), TOK)


def join_kernel(place_ref, *refs):
    x, z = place_ref[0], place_ref[1]
    outs = refs[GROUP:]
    for source in range(GROUP):
        place = lax.rem(x + source, SIDE) if source < SIDE else SIDE
        for step in range(SIDE):
            outs[step][:, column(place)] = refs[source][rows_of(z, source, step)]


def channels_kernel(place_ref, *refs):
    x, z = place_ref[0], place_ref[1]
    cots = refs[GROUP : GROUP + SIDE]
    chan_ref = refs[GROUP + SIDE]
    chan_ref[...] = jnp.zeros_like(chan_ref)
    for source in range(GROUP):
        place = lax.rem(x + source, SIDE) if source < SIDE else SIDE
        total = jnp.zeros((TOK, HEAD_DIM), jnp.float32)
        for step in range(SIDE):
            attn = refs[source][rows_of(z, source, step)].astype(jnp.float32)
            total = total + attn * cots[step][:, column(place)].astype(jnp.float32)
        chan_ref[pl.ds(place, 1)] = jnp.sum(total, axis=0, keepdims=True)


def spread_kernel(chan_ref, time_ref, out_ref):
    for i in range(out_ref.shape[0]):
        out_ref[i] = chan_ref[...]
        out_ref[i, GROUP : GROUP + 1] = time_ref[...]


def finish_kernel(z_ref, a0, a1, a2, a3, gate_ref, out_ref):
    z = z_ref[0]
    for step, a in enumerate((a0, a1, a2, a3)):
        cols = group_columns(z + step)
        out_ref[:, cols] = (a[...].astype(jnp.float32) * gate_ref[:, cols]).astype(jnp.bfloat16)


def grad_kernel(index_ref, freq_ref, before_ref, chan_ref, out_ref):
    is_cosine = index_ref[0] < FREQS // 2
    factors = []
    for d in range(SIDE):
        angle = chan_ref[d, GROUP : GROUP + 1] * freq_ref[...]
        factors.append(jnp.where(is_cosine, jnp.cos(angle), jnp.sin(angle)))
    for z in range(SIDE):
        chans = [sum(chan_ref[(x * SIDE + z) * SIDE + d] for x in range(SIDE)) for d in range(SIDE)]
        for head in range(GROUP):
            total = sum(f * c[head : head + 1] for f, c in zip(factors, chans, strict=True))
            at = (z * GROUP + head) * HEAD_DIM
            cols = slice(at, at + HEAD_DIM)
            out_ref[:, cols] = before_ref[...] + total


def shape(dims, dtype=jnp.bfloat16):
    return jax.ShapeDtypeStruct(dims, dtype)


def frequencies():
    count = FREQS // 2
    return (10000.0 ** (-np.arange(count) / count)).astype(np.float32)


def embed(step):
    angle = step.astype(jnp.float32) * frequencies()
    return jnp.concatenate([jnp.cos(angle), jnp.sin(angle)])


def local(qkv, qk_gain, mod_weight, positions, timesteps, cotangent):
    ctx = lax.axis_index("ctx").astype(jnp.int32)
    x = (ctx // SIDE)[None]
    z = (ctx % SIDE)[None]
    steps = (1, 2, 3)
    place = jnp.concatenate([x, z])
    count = SIDE * SIDE
    block = shape((3, TOK, HEAD_DIM))
    single = shape((ROWS, HEAD_DIM))
    flat = shape((TOK, GROUP * HEAD_DIM))

    step = timesteps[0, 0]
    when = jnp.full((1, HEAD_DIM), step.astype(jnp.float32))
    gains = lax.ppermute(qk_gain[0], "segment", [((i + 1) % SIDE, i) for i in range(SIDE)])
    parts = qkv[0, 0].transpose(1, 0, 2)
    cots = call(cut_cotangent_kernel, [flat] * SIDE, 0, 1_600_000, z, cotangent[0, 0])
    cots_z = [None] * SIDE
    for k in (2, 1):
        cots_z[k] = away(cots[k], k)
    cosine, sine = rope_tables(positions[0])
    main, *shared = call(
        prep_kernel,
        [shape((count, 3, TOK, HEAD_DIM))] + [block] * SIDE,
        10_000_000,
        5_000_000,
        z,
        parts,
        gains,
        cosine,
        sine,
    )
    shared_z = exchanged(along_z, shared)
    main = lax.all_to_all(after(main, shared_z), "ctx", 0, 0)
    pair = jnp.concatenate([b[1:] for b in shared_z], axis=1)
    pairs = [pair] + [along_x(pair, k) for k in steps]
    gate = jnp.dot(embed(step), mod_weight[0], precision=lax.Precision.HIGHEST)[None]
    rows = FREQS // (SIDE * SIDE * SIDE)
    index = (ctx * SIDE + lax.axis_index("dp").astype(jnp.int32)) * rows
    freq = lax.dynamic_slice_in_dim(np.tile(frequencies(), 2), index, rows)
    freq = jnp.broadcast_to(freq[:, None], (rows, HEAD_DIM))
    shared_out = call(
        shared_kernel, single, 840_000_000, 1_600_000, *shared_z, *pairs, smem=0
    )
    main, gate, freq = lax.optimization_barrier((main, gate, freq))
    back = [None] * SIDE
    back[2], back[1], back[3] = call(
        functools.partial(main_kernel, (2, 1, 3)), [single] * 3, 2_500_000_000, 2_500_000, x, main
    )
    (back[0],) = call(
        functools.partial(main_kernel, (0,)), [single], 840_000_000, 2_000_000, x, main
    )
    for k in (3, 0):
        cots_z[k] = away(after(cots[k], back[2]), k)
    back = [back[0]] + [along_x(back[m], SIDE - m) for m in steps]
    joined = call(
        join_kernel, [flat] * SIDE, 0, 1_600_000, place, *back, after(shared_out, cots_z[1:3])
    )
    at_home = [None] * SIDE
    for k in (2, 1, 3, 0):
        at_home[k] = home(joined[k], (SIDE - k) % SIDE)

    chan = call(
        channels_kernel, shape((8, HEAD_DIM), jnp.float32), 0, 0, place, *back, shared_out, *cots_z
    )
    chan = home(chan, 0)

    def gradient(_, state):
        mine, before = lax.optimization_barrier((chan, state[1]))
        chans = call(
            spread_kernel, shape((SIDE * count, 8, HEAD_DIM), jnp.float32), 0, 0, mine, when, smem=0
        )
        chans = lax.all_to_all(chans, ("ctx", "dp"), 0, 0)
        grad = call(grad_kernel, zeros, 0, 200_000, index[None], freq, before, chans)
        return (grad, before)

    zeros = shape((rows, WIDTH), jnp.float32)
    turns = jnp.where(step < 1000, 1, 2)
    start = (jnp.zeros((rows, WIDTH), jnp.float32), jnp.zeros((rows, HEAD_DIM), jnp.float32))
    grad, _ = lax.fori_loop(0, turns, gradient, start)

    attn_out = call(
        finish_kernel, shape((TOK, WIDTH)), 500_000, 1_700_000, z, *after(at_home, grad), gate
    )
    return (attn_out[None, None], grad[None])


def solution(mesh):
    return jax.shard_map(
        local,
        mesh=mesh,
        in_specs=(
            P("segment", "dp", "ctx", None, None),
            P("segment", None, None),
            P("segment", None, None),
            P("dp", "ctx"),
            P("segment", "dp"),
            P("segment", "dp", "ctx", None),
        ),
        out_specs=(P("segment", "dp", "ctx", None), P("segment", ("ctx", "dp"), None)),
        check_vma=False,
    )
```

```python
import functools

import jax
import jax.numpy as jnp
import numpy as np
from jax import lax
from jax.experimental import pallas as pl
from jax.experimental.pallas import tpu as pltpu
from jax.sharding import PartitionSpec as P

HEADS = 20
HEAD_DIM = 128
FREQS = 256
GRID_ROWS = 45
GRID_COLS = 80
SIDE = 4
GROUP = HEADS // SIDE
TOK = 160
ROWS = SIDE * TOK
WIDTH = HEADS * HEAD_DIM
TILE = 320
EXP_SCALE = 1.4426950408889634 / HEAD_DIM**0.5
VMEM = pltpu.CompilerParams(vmem_limit_bytes=56 * 1024 * 1024)
SMEM_SPEC = pl.BlockSpec(memory_space=pltpu.SMEM)
VMEM_SPEC = pl.BlockSpec(memory_space=pltpu.VMEM)


def along_z(value, by):
    pairs = [(i, i // SIDE * SIDE + (i + by) % SIDE) for i in range(SIDE * SIDE)]
    return lax.ppermute(value, "ctx", pairs)


def along_x(value, by):
    pairs = [(i, (i + SIDE * by) % (SIDE * SIDE)) for i in range(SIDE * SIDE)]
    return lax.ppermute(value, "ctx", pairs)


def along_dp(value, by):
    return lax.ppermute(value, "dp", [(i, (i + by) % SIDE) for i in range(SIDE)])


def exchanged(along, blocks):
    got = list(blocks)
    for k in (2, 1, 3):
        got[k] = along(blocks[k], k)
    return got


def section_pairs(turn, by):
    count = SIDE * SIDE
    pairs = []
    for seg in range(SIDE):
        for i in range(count):
            target = (seg + turn) % SIDE * count + i // SIDE * SIDE + (i + by) % SIDE
            pairs.append((seg * count + i, target))
    return pairs


def home(value, by):
    return lax.ppermute(value, ("segment", "ctx"), section_pairs(1, by))


def away(value, by):
    return lax.ppermute(value, ("segment", "ctx"), section_pairs(SIDE - 1, by))


def rope_tables(pos):
    half = HEAD_DIM // 2
    side = HEAD_DIM // 6
    first = half - 2 * side
    frame = (pos // (GRID_ROWS * GRID_COLS)).astype(jnp.float32)
    row = (pos // GRID_COLS % GRID_ROWS).astype(jnp.float32)
    col = (pos % GRID_COLS).astype(jnp.float32)
    pair = np.arange(half)
    group = np.where(pair < first, 0, np.where(pair < first + side, 1, 2))
    offset = np.where(group == 0, 0, np.where(group == 1, first, first + side))
    pairs_in = np.where(group == 0, first, side)
    freq = (10000.0 ** (-(pair - offset) / pairs_in)).astype(np.float32)
    coord = jnp.where(
        group[None, :] == 0,
        frame[:, None],
        jnp.where(group[None, :] == 1, row[:, None], col[:, None]),
    )
    angle = coord * freq[None, :]
    cosine = jnp.concatenate([jnp.cos(angle), jnp.cos(angle)], axis=1)
    sine = jnp.concatenate([-jnp.sin(angle), jnp.sin(angle)], axis=1)
    return (cosine, sine)


def one_of(which, dims):
    return pl.BlockSpec((1, *dims), lambda i: (which, 0, 0))


def call(kernel, out_shape, flops, moved, *operands, smem=1, specs=None):
    grid = () if specs is None else (1,)
    specs = specs or [SMEM_SPEC] * smem + [VMEM_SPEC] * (len(operands) - smem)
    return pl.pallas_call(
        kernel,
        grid=grid,
        out_shape=out_shape,
        in_specs=specs,
        out_specs=jax.tree.map(lambda _: VMEM_SPEC, out_shape),
        compiler_params=VMEM,
        cost_estimate=pl.CostEstimate(flops=0, bytes_accessed=0, transcendentals=0),
    )(*operands)


def group_columns(index):
    wide = GROUP * HEAD_DIM
    return pl.ds(pl.multiple_of(lax.rem(index, SIDE) * wide, HEAD_DIM), wide)


def after(value, first):
    return lax.optimization_barrier((value, first))[0]


def column(index):
    return pl.ds(pl.multiple_of(index * HEAD_DIM, HEAD_DIM), HEAD_DIM)


def prep_kernel(z_ref, qkv_ref, gain_ref, cos_ref, sin_ref, main_ref, *shared):
    z = z_ref[0]
    cosine = cos_ref[...]
    sine = sin_ref[...]
    for part in range(3):
        if part < 2:
            total = jnp.zeros((TOK, HEAD_DIM), jnp.float32)
            for head in range(HEADS):
                x = qkv_ref[part, :, head * HEAD_DIM : (head + 1) * HEAD_DIM].astype(jnp.float32)
                total = total + x * x
            mean_sq = jnp.sum(total, axis=1, keepdims=True) / WIDTH
            inverse = lax.rsqrt(mean_sq + 1e-06)

        def head_of(cols):
            x = qkv_ref[part, :, cols]
            if part == 2:
                return x
            y = x.astype(jnp.float32) * inverse * gain_ref[part : part + 1, cols]
            turned = pltpu.roll(y, HEAD_DIM // 2, 1)
            return (y * cosine + turned * sine).astype(jnp.bfloat16)

        for step in range(SIDE):
            shared[step][part] = head_of(column(lax.rem(z + step, SIDE) * GROUP + GROUP - 1))
        for to_x in range(SIDE):
            for to_z in range(SIDE):
                at = (to_z * GROUP + to_x) * HEAD_DIM
                main_ref[to_x * SIDE + to_z, part] = head_of(slice(at, at + HEAD_DIM))


def cut_cotangent_kernel(z_ref, cot_ref, *outs):
    z = z_ref[0]
    for step in range(SIDE):
        outs[step][...] = cot_ref[:, group_columns(z + step)]


def attend(q, keys, values):
    nt = (((1,), (1,)), ((), ()))
    scores = [lax.dot_general(q, k, nt, preferred_element_type=jnp.float32) for k in keys]
    peak = functools.reduce(jnp.maximum, [jnp.max(s, axis=1, keepdims=True) for s in scores])
    expo = [jnp.exp2((s - peak) * EXP_SCALE) for s in scores]
    total = sum(jnp.sum(e, axis=1, keepdims=True) for e in expo)
    accum = sum(
        jnp.dot(e.astype(jnp.bfloat16), v, preferred_element_type=jnp.float32)
        for e, v in zip(expo, values, strict=True)
    )
    return (accum / total).astype(jnp.bfloat16)


def shared_kernel(q0, q1, q2, q3, s0, s1, s2, s3, out_ref):
    blocks = (s0, s1, s2, s3)
    for pair in ((q0, q1), (q2, q3)):
        at = 0 if pair[0] is q0 else TILE
        q = jnp.concatenate([p[0] for p in pair])
        out_ref[at : at + TILE] = attend(q, [b[0] for b in blocks], [b[1] for b in blocks])


def main_kernel(back, x_ref, r_ref, *outs):
    x = x_ref[0]

    def four(part, first):
        return r_ref[pl.ds(first * SIDE, SIDE), part].reshape(ROWS, HEAD_DIM)

    keys = [four(1, m) for m in range(SIDE)]
    values = [four(2, m) for m in range(SIDE)]
    for step, out_ref in zip(back, outs, strict=True):
        first = lax.rem(x + SIDE - step, SIDE) * SIDE
        for i in range(ROWS // TILE):
            half = SIDE // 2
            q = r_ref[pl.ds(first + i * half, half), 0].reshape(TILE, HEAD_DIM)
            out_ref[i * TILE : (i + 1) * TILE] = attend(q, keys, values)


def rows_of(z, source, step):
    first = lax.rem(z + SIDE - step, SIDE) if source < SIDE else step
    return pl.ds(pl.multiple_of(first * TOK, 32), TOK)


def join_kernel(place_ref, *refs):
    x, z = place_ref[0], place_ref[1]
    outs = refs[GROUP:]
    for source in range(GROUP):
        place = lax.rem(x + source, SIDE) if source < SIDE else SIDE
        for step in range(SIDE):
            outs[step][:, column(place)] = refs[source][rows_of(z, source, step)]


def channels_kernel(place_ref, time_ref, *refs):
    x, z = place_ref[0], place_ref[1]
    cots = refs[GROUP : GROUP + SIDE]
    out_ref, chan_ref = refs[GROUP + SIDE :]
    chan_ref[...] = jnp.zeros_like(chan_ref)
    for source in range(GROUP):
        place = lax.rem(x + source, SIDE) if source < SIDE else SIDE
        total = jnp.zeros((TOK, HEAD_DIM), jnp.float32)
        for step in range(SIDE):
            attn = refs[source][rows_of(z, source, step)].astype(jnp.float32)
            total = total + attn * cots[step][:, column(place)].astype(jnp.float32)
        chan_ref[pl.ds(place, 1)] = jnp.sum(total, axis=0, keepdims=True)
    chan_ref[GROUP : GROUP + 1] = time_ref[2:3, :HEAD_DIM]
    for i in range(out_ref.shape[0]):
        out_ref[i] = chan_ref[...]


def finish_kernel(z_ref, a0, a1, a2, a3, gate_ref, out_ref):
    z = z_ref[0]
    for step, a in enumerate((a0, a1, a2, a3)):
        cols = group_columns(z + step)
        out_ref[:, cols] = (a[...].astype(jnp.float32) * gate_ref[:, cols]).astype(jnp.bfloat16)


def grad_kernel(index_ref, freq_ref, before_ref, chan_ref, out_ref):
    is_cosine = index_ref[0] < FREQS // 2
    factors = []
    for d in range(SIDE):
        angle = chan_ref[d, GROUP : GROUP + 1] * freq_ref[...]
        factors.append(jnp.where(is_cosine, jnp.cos(angle), jnp.sin(angle)))
    for z in range(SIDE):
        chans = [sum(chan_ref[(x * SIDE + z) * SIDE + d] for x in range(SIDE)) for d in range(SIDE)]
        for head in range(GROUP):
            total = sum(f * c[head : head + 1] for f, c in zip(factors, chans, strict=True))
            at = (z * GROUP + head) * HEAD_DIM
            cols = slice(at, at + HEAD_DIM)
            out_ref[:, cols] = before_ref[...] + total


def shape(dims, dtype=jnp.bfloat16):
    return jax.ShapeDtypeStruct(dims, dtype)


def frequencies():
    count = FREQS // 2
    return (10000.0 ** (-np.arange(count) / count)).astype(np.float32)


def embed(step):
    angle = step.astype(jnp.float32) * frequencies()
    return jnp.concatenate([jnp.cos(angle), jnp.sin(angle)])


def local(qkv, qk_gain, mod_weight, positions, timesteps, cotangent):
    ctx = lax.axis_index("ctx").astype(jnp.int32)
    x = (ctx // SIDE)[None]
    z = (ctx % SIDE)[None]
    steps = (1, 2, 3)
    place = jnp.concatenate([x, z])
    count = SIDE * SIDE
    block = shape((3, TOK, HEAD_DIM))
    single = shape((ROWS, HEAD_DIM))
    flat = shape((TOK, GROUP * HEAD_DIM))

    step = timesteps[0, 0]
    when = jnp.full((1, WIDTH), step.astype(jnp.float32))
    gains = jnp.concatenate([qk_gain[0], when])
    gains = lax.ppermute(gains, "segment", [((i + 1) % SIDE, i) for i in range(SIDE)])
    parts = qkv[0, 0].transpose(1, 0, 2)
    cots = call(cut_cotangent_kernel, [flat] * SIDE, 0, 1_600_000, z, cotangent[0, 0])
    cots_z = [None] * SIDE
    for k in (2, 1):
        cots_z[k] = away(cots[k], k)
    cosine, sine = rope_tables(positions[0])
    main, *shared = call(
        prep_kernel,
        [shape((count, 3, TOK, HEAD_DIM))] + [block] * SIDE,
        10_000_000,
        5_000_000,
        z,
        parts,
        gains,
        cosine,
        sine,
    )
    shared_z = exchanged(along_z, shared)
    main = lax.all_to_all(after(main, shared_z), "ctx", 0, 0)
    pair = jnp.concatenate([b[1:] for b in shared_z], axis=1)
    pairs = [pair] + [along_x(pair, k) for k in steps]
    gate = jnp.dot(embed(step), mod_weight[0], precision=lax.Precision.HIGHEST)[None]
    rows = FREQS // (SIDE * SIDE * SIDE)
    index = (ctx * SIDE + lax.axis_index("dp").astype(jnp.int32)) * rows
    freq = lax.dynamic_slice_in_dim(np.tile(frequencies(), 2), index, rows)
    freq = jnp.broadcast_to(freq[:, None], (rows, HEAD_DIM))
    shared_out = call(
        shared_kernel, single, 840_000_000, 1_600_000, *shared_z, *pairs, smem=0
    )
    main, gate, freq = lax.optimization_barrier((main, gate, freq))
    back = [None] * SIDE
    back[2], back[1], back[3] = call(
        functools.partial(main_kernel, (2, 1, 3)), [single] * 3, 2_500_000_000, 2_500_000, x, main
    )
    (back[0],) = call(
        functools.partial(main_kernel, (0,)), [single], 840_000_000, 2_000_000, x, main
    )
    for k in (3, 0):
        cots_z[k] = away(after(cots[k], back[2]), k)
    back = [back[0]] + [along_x(back[m], SIDE - m) for m in steps]
    joined = call(
        join_kernel, [flat] * SIDE, 0, 1_600_000, place, *back, after(shared_out, cots_z[1:3])
    )
    at_home = [None] * SIDE
    for k in (2, 1, 3, 0):
        at_home[k] = home(joined[k], (SIDE - k) % SIDE)

    def gradient(_, state):
        attn, before = lax.optimization_barrier(([*back, shared_out], state[1]))
        chans = pl.pallas_call(
            channels_kernel,
            out_shape=shape((SIDE * count, 8, HEAD_DIM), jnp.float32),
            in_specs=[SMEM_SPEC] + [VMEM_SPEC] * (1 + GROUP + SIDE),
            out_specs=VMEM_SPEC,
            scratch_shapes=[pltpu.VMEM((8, HEAD_DIM), jnp.float32)],
            compiler_params=VMEM,
            cost_estimate=pl.CostEstimate(flops=0, bytes_accessed=0, transcendentals=0),
        )(place, gains, *attn, *cots_z)
        chans = lax.all_to_all(chans, ("ctx", "dp"), 0, 0)
        grad = call(grad_kernel, zeros, 0, 200_000, index[None], freq, before, chans)
        return (grad, before)

    zeros = shape((rows, WIDTH), jnp.float32)
    start = (jnp.zeros((rows, WIDTH), jnp.float32), jnp.zeros((rows, HEAD_DIM), jnp.float32))
    grad, _ = gradient(0, start)
    grad = lax.ppermute(grad, "segment", [(i, (i + 1) % SIDE) for i in range(SIDE)])

    attn_out = call(
        finish_kernel, shape((TOK, WIDTH)), 500_000, 1_700_000, z, *at_home, gate
    )
    return (attn_out[None, None], grad[None])


def solution(mesh):
    return jax.shard_map(
        local,
        mesh=mesh,
        in_specs=(
            P("segment", "dp", "ctx", None, None),
            P("segment", None, None),
            P("segment", None, None),
            P("dp", "ctx"),
            P("segment", "dp"),
            P("segment", "dp", "ctx", None),
        ),
        out_specs=(P("segment", "dp", "ctx", None), P("segment", ("ctx", "dp"), None)),
        check_vma=False,
    )
```
